512 devices in a mesh: sweep: 4 (over y), ops: 128 (over z, x, core).
Axes of the slice: x: 4, y: 4, z: 16, core: 2. Of those that a mesh axis runs over, the one named last changes fastest.
Arguments:
- initial_trial_state: bfloat16 [4, 32, 128, 128], P('sweep'), may hold values from -6 to 6
- left_ops: bfloat16 [4, 128, 32, 128, 128], P('sweep', 'ops'), may hold values from -0.5 to 0.5
- right_ops: bfloat16 [4, 128, 32, 128, 128], P('sweep', 'ops'), may hold values from -0.5 to 0.5
- pair_sectors: int32 [4, 128, 32], P('sweep', 'ops'), may hold values 0 or 1
- sector_size: int32 [4, 32], P('sweep'), may hold values from 1 to 128, 3072 in all within a row
- left_env: bfloat16 [4, 32, 128, 128], P('sweep'), may hold values from -0.5 to 0.5
Outputs:
- psi_out: bfloat16 [4, 32, 128, 128], P('sweep')
- next_left: bfloat16 [4, 32, 128, 128], P('sweep')
The draws below stay inside these ranges and needn't reach their ends.
Inputs may be any that keep to these rules, and one draw needn't show every extreme that they name: `sector_size`: at each position the sector sizes sum to 3072 and the largest is exactly 128.
All inputs are finite; a program needn't handle non-finite values. No bound on the sum of `pair_sectors` on one device may be relied on, other than what follows from the above.
Results may differ from the reference program's by a relative error of at most 0.012.
Values may be sent and summed in bfloat16 or wider, within the bound.
No kernel may reach another device: no remote copies, remote signals or barrier semaphores. Data moves between devices by JAX's collectives and lax.ppermute only.
A program may use at most 64 MiB of HBM per device.

```python
import math
import jax
import jax.numpy as jnp
import numpy as np
from jax import lax

NB = 32
B = 128
ITERS = 2
PAIRS = 128
POS = 4


def place_ends(result, stream_key, smallest, high):
    longest = result.shape.index(max(result.shape))
    spots = []
    for shift in (0, 1):
        where = [jax.random.randint(jax.random.fold_in(stream_key, axis), (), 0, length) for axis, length in enumerate(result.shape)]
        where[longest] = (where[longest] + shift) % result.shape[longest]
        spots.append(tuple(where))
    return result.at[spots[0]].set(smallest).at[spots[1]].set(high)


def level_of(stream_key, dims, shards, low, top_value):
    loudness, own = 1.0, jax.random.fold_in(stream_key, 6)
    for position, parts in shards:
        heights = jnp.exp(jax.random.uniform(jax.random.fold_in(own, position), (parts,), jnp.float32, low / len(shards), top_value / len(shards)))
        loudness = loudness * jnp.repeat(heights, dims[position] // parts).reshape([-1 if axis == position else 1 for axis in range(len(dims))])
    return loudness


def length_profile(amount, total, limit, slope):
    loads = [(1 << 20) // math.isqrt(grade ** slope) + 1 for grade in range(2, amount + 1)]
    rest, holding = total - limit - (amount - 1), [1] * (amount - 1)
    while rest > 0:
        candidates = [i for i in range(amount - 1) if holding[i] < limit]
        mass, left = sum([loads[i] for i in candidates]), rest
        for i in candidates:
            extra = min(limit - holding[i], max(1, left * loads[i] // mass), rest)
            holding[i] = holding[i] + extra
            rest = rest - extra
    return np.array([limit] + holding)


def uneven_parts(stream_key, amount, total, most, lean):
    if amount == 2:
        one = jax.random.randint(stream_key, (), max(1, total - most), min(most, total - 1) + 1)
        return jnp.stack([one, total - one])
    sizes = jnp.asarray(length_profile(amount, total, most, lean), jnp.int32)
    twos = (amount - 1) // 2
    source_of, sink = sizes[1:1 + 2 * twos:2], sizes[2:2 + 2 * twos:2]
    slack = jnp.minimum(source_of - 1, most - sink)
    passed = jax.random.randint(jax.random.fold_in(stream_key, 1), (twos,), 0, 1 << 20) % (slack + 1)
    sizes = sizes.at[1:1 + 2 * twos:2].set(source_of - passed).at[2:2 + 2 * twos:2].set(sink + passed)
    return sizes[jax.random.permutation(jax.random.fold_in(stream_key, 2), amount)]


def gaussian(stream_key, shape, width, most, cuts=(), held_as=jnp.bfloat16):
    loudness = level_of(stream_key, shape, cuts, -0.22, 0.18) if cuts else 1.0
    result = jax.random.normal(stream_key, shape, jnp.float32) * width * loudness
    return jnp.minimum(jnp.maximum(result, -most), most).astype(held_as)


def setup_inputs(seed: int = 0) -> dict:
    seeds = jax.random.split(jax.random.key(seed), 7)
    return {
        "initial_trial_state": gaussian(seeds[0], (POS, NB, B, B), 1.0, 6.0, ((0, 4),)),
        "left_ops": gaussian(seeds[1], (POS, PAIRS, NB, B, B), B ** -0.5, 0.5, ((0, 4), (1, 128))),
        "right_ops": gaussian(seeds[2], (POS, PAIRS, NB, B, B), B ** -0.5, 0.5, ((0, 4), (1, 128))),
        "pair_sectors": place_ends((jax.random.randint(seeds[3], (POS, PAIRS, NB), 0, 4) < 3).astype(jnp.int32), jax.random.fold_in(seeds[3], 1), 0, 1),
        "sector_size": jax.vmap(lambda own: uneven_parts(own, NB, 3 * NB * B // 4, B, 2))(jax.random.split(seeds[4], POS)).reshape((POS, NB)).astype(jnp.int32),
        "left_env": gaussian(seeds[5], (POS, NB, B, B), B ** -0.5, 0.5, ((0, 4),)),
    }


def sector_mask(sizes):
    live = jnp.arange(B)[None, :] < sizes[:, None]
    return (live[:, :, None] & live[:, None, :]).astype(jnp.float32)

def rounded(value):
    return lax.optimization_barrier(value.astype(jnp.bfloat16)).astype(jnp.float32)

def reference(initial_trial_state, left_ops, right_ops, pair_sectors, sector_size, left_env):
    scale = 1.0 / math.sqrt(PAIRS)
    output_wavefunctions = []
    results_rescaled = []
    for spot in range(POS):
        weight = sector_mask(sector_size[spot])
        env = left_env[spot].astype(jnp.float32)
        x = weight * initial_trial_state[spot].astype(jnp.float32)
        for step in range(ITERS):
            xb = rounded(x)

            def add_pair(total, item):
                left, right_environment, live = item
                left_f = left.astype(jnp.float32)
                east_context_precise = right_environment.astype(jnp.float32)
                live_f = live.astype(jnp.float32)[:, None, None]
                front_multiplier = rounded(live_f * jnp.einsum('iab,ibc->iac', left_f, xb))
                rear_multiplier = rounded(live_f * jnp.einsum('iba,ibc->iac', left_f, xb))
                summand_piece = jnp.einsum('cfy,cdy->cfd', front_multiplier, east_context_precise) + jnp.einsum('ylr,yre->yle', rear_multiplier, east_context_precise)
                return (total + summand_piece, None)
            start = jnp.zeros((NB, B, B), jnp.float32)
            collapsed_aggregate, _ = lax.scan(add_pair, start, (left_ops[spot], right_ops[spot], pair_sectors[spot]))
            sigma = weight * (scale * collapsed_aggregate + jnp.einsum('iab,ibc->iac', env, xb))
            rho = jnp.sum(x * sigma) / jnp.sum(x * x)
            y_new = x - 0.8 * (sigma - rho * x)
            x = y_new / jnp.sqrt(jnp.sum(y_new * y_new) / (NB * B * B) + 1e-06)
        psi_b = x.astype(jnp.bfloat16)
        psi_f = psi_b.astype(jnp.float32)
        applied = rounded(jnp.einsum('iab,ibc->iac', env, psi_f))
        normalize_again = jnp.einsum('iba,ibc->iac', psi_f, applied) / math.sqrt(B)
        output_wavefunctions.append(psi_b)
        results_rescaled.append(normalize_again.astype(jnp.bfloat16))
    lefts = []
    for spot in range(POS):
        env = left_env[spot].astype(jnp.float32)
        if spot > 0:
            env = env + results_rescaled[spot - 1].astype(jnp.float32)
        lefts.append(env.astype(jnp.bfloat16))
    return (jnp.stack(output_wavefunctions), jnp.stack(lefts))
```

```python
import math

import jax
import jax.numpy as jnp
from jax import lax
from jax.experimental import pallas as pl
from jax.experimental.pallas import tpu as pltpu
from jax.sharding import Mesh, PartitionSpec as P

ITERS = 2
NSEC = 32
WIDTH = 128
PAIRS = 128
ROWS = 3 * NSEC * WIDTH // 4
HALF = ROWS // 2
TOTAL = NSEC * WIDTH * WIDTH
X, ZL, ZH = 4, 4, 4
NEAR = ZL * X
PIECE = HALF // NEAR
SCALE = 1.0 / math.sqrt(PAIRS)

WHOLE = pl.BlockSpec(memory_space=pltpu.VMEM)
SCALARS = pl.BlockSpec(memory_space=pltpu.SMEM)


def square_mask(size):
    row = lax.broadcasted_iota(jnp.int32, (WIDTH, WIDTH), 0)
    col = lax.broadcasted_iota(jnp.int32, (WIDTH, WIDTH), 1)
    return (row < size) & (col < size)


def dot(a, b, left_dim, right_dim):
    return lax.dot_general(
        a, b, (((left_dim,), (right_dim,)), ((), ())), preferred_element_type=jnp.float32
    )


def fold(value):
    return jnp.sum(value.reshape(WIDTH // 8, 8, WIDTH), axis=0)


def step_factors(sizes, x_of, sigma, masked):
    def body(i, carry):
        offset, xx, xs, ss = carry
        size = sizes[i]
        x = x_of(i)
        s = jnp.where(square_mask(size), sigma[pl.ds(offset, WIDTH), :], 0.0)
        masked[i] = s
        return offset + size, xx + fold(x * x), xs + fold(x * s), ss + fold(s * s)

    zero = jnp.zeros((8, WIDTH), jnp.float32)
    _, xx, xs, ss = lax.fori_loop(0, NSEC, body, (jnp.int32(0), zero, zero, zero), unroll=2)
    xx, xs, ss = jnp.sum(xx), jnp.sum(xs), jnp.sum(ss)
    rho = xs / xx
    yy = xx + 0.64 * jnp.maximum(ss - rho * xs, 0.0)
    shrink = 1.0 / jnp.sqrt(jnp.full((8, WIDTH), yy / TOTAL + 1e-06))[0, 0]
    return (1.0 + 0.8 * rho) * shrink, 0.8 * shrink


def pair_sum(meta, sizes, live, xb_of, left, right, env, packed, mine, other):
    sector = meta[1]

    def body(i, offset):
        xb = xb_of(i)
        on = live[i].astype(jnp.float32)
        block = left[i]
        front = (on * dot(block, xb, 1, 0)).astype(jnp.bfloat16)
        rear = (on * dot(block, xb, 0, 0)).astype(jnp.bfloat16)
        context = right[i]
        total = SCALE * (dot(front, context, 1, 1) + dot(rear, context, 1, 0))
        packed[pl.ds(offset, WIDTH), :] = total

        @pl.when(i == sector)
        def _():
            packed[pl.ds(offset, WIDTH), :] += 0.25 * dot(env[0], xb, 1, 0)

        return offset + sizes[i]

    lax.fori_loop(0, NSEC, body, jnp.int32(0), unroll=2)
    core = meta[0]
    mine[...] = packed[pl.ds(pl.multiple_of(core * HALF, 8), HALF), :]
    other[...] = packed[pl.ds(pl.multiple_of((1 - core) * HALF, 8), HALF), :].astype(jnp.bfloat16)


def first_kernel(meta, sizes, live, x0, left, right, env, mine, other, packed):
    def xb_of(i):
        x = x0[i]
        return jnp.where(square_mask(sizes[i]), x, jnp.zeros_like(x))

    pair_sum(meta, sizes, live, xb_of, left, right, env, packed, mine, other)


def next_kernel(meta, sizes, live, x0, sigma, left, right, env, mine, other, x_out, packed, wide, masked):
    def x_of(i):
        return jnp.where(square_mask(sizes[i]), x0[i].astype(jnp.float32), 0.0)

    wide[pl.ds(0, ROWS), :] = sigma[...].astype(jnp.float32)
    grow, drop = step_factors(sizes, x_of, wide, masked)

    def xb_of(i):
        x = grow * x_of(i) - drop * masked[i]
        x_out[i] = x
        return x.astype(jnp.bfloat16)

    pair_sum(meta, sizes, live, xb_of, left, right, env, packed, mine, other)


def last_kernel(sizes, x, sigma, env, psi_out, renorm_out, wide, masked):
    def x_of(i):
        return x[i]

    wide[pl.ds(0, ROWS), :] = sigma[...].astype(jnp.float32)
    grow, drop = step_factors(sizes, x_of, wide, masked)

    def body(i, carry):
        psi = (grow * x_of(i) - drop * masked[i]).astype(jnp.bfloat16)
        psi_out[i] = psi
        applied = dot(env[i], psi, 1, 0).astype(jnp.bfloat16)
        renorm_out[i] = (dot(psi, applied, 0, 0) / math.sqrt(WIDTH)).astype(jnp.bfloat16)
        return carry

    lax.fori_loop(0, NSEC, body, 0, unroll=2)


def shape(dims, dtype):
    return jax.ShapeDtypeStruct(dims, dtype)


PACKED = pltpu.VMEM((ROWS + WIDTH, WIDTH), jnp.float32)
BLOCKS = pltpu.VMEM((NSEC, WIDTH, WIDTH), jnp.float32)
PARAMS = pltpu.CompilerParams(vmem_limit_bytes=32 * 1024 * 1024)


def one_sector(meta, sizes, live):
    return pl.BlockSpec((1, WIDTH, WIDTH), lambda i, meta, sizes, live: (meta[1], 0, 0))


def pair_call(kernel, extra, out_extra, scratch):
    return pl.pallas_call(
        kernel,
        grid_spec=pltpu.PrefetchScalarGridSpec(
            num_scalar_prefetch=3,
            grid=(1,),
            in_specs=[WHOLE] * (3 + extra)
            + [pl.BlockSpec((1, WIDTH, WIDTH), lambda i, meta, sizes, live: (meta[1], 0, 0))],
            out_specs=[WHOLE] * (2 + len(out_extra)),
            scratch_shapes=scratch,
        ),
        out_shape=[shape((HALF, WIDTH), jnp.float32), shape((HALF, WIDTH), jnp.bfloat16)] + out_extra,
        compiler_params=PARAMS,
    )


def exchange(value, axes):
    return lax.all_to_all(value, axes, 0, 0)


def all_summed(mine, other):
    came = lax.ppermute(other, "core", [(0, 1), (1, 0)])
    chip = (mine + came.astype(jnp.float32)).astype(jnp.bfloat16).reshape(NEAR, PIECE, WIDTH)
    near = jnp.sum(exchange(chip, ("zl", "x")).astype(jnp.float32), axis=0).astype(jnp.bfloat16)
    far = exchange(jnp.broadcast_to(near[None], (ZH, PIECE, WIDTH)), "zh")
    piece = jnp.sum(far.astype(jnp.float32), axis=0).astype(jnp.bfloat16)
    half = exchange(jnp.broadcast_to(piece[None], (NEAR, PIECE, WIDTH)), ("zl", "x"))
    return lax.all_gather(half.reshape(HALF, WIDTH), "core", tiled=True)


def shards(initial_trial_state, left_ops, right_ops, pair_sectors, sector_size, left_env):
    x0 = initial_trial_state[0]
    left = left_ops[0, 0]
    right = right_ops[0, 0]
    live = pair_sectors[0, 0]
    sizes = sector_size[0]
    env = left_env[0]
    core = lax.axis_index("core")
    sector = lax.axis_index(("zh", "zl", "x", "core")) // (PAIRS // NSEC)
    meta = jnp.stack([core, sector]).astype(jnp.int32)

    mine, other = pair_call(first_kernel, 0, [], [PACKED])(meta, sizes, live, x0, left, right, env)
    sigma = all_summed(mine, other)
    mine, other, x = pair_call(
        next_kernel, 1, [shape((NSEC, WIDTH, WIDTH), jnp.float32)], [PACKED, PACKED, BLOCKS]
    )(meta, sizes, live, x0, sigma, left, right, env)
    sigma = all_summed(mine, other)
    psi, renorm = pl.pallas_call(
        last_kernel,
        in_specs=[SCALARS] + [WHOLE] * 3,
        out_specs=[WHOLE] * 2,
        out_shape=[shape((NSEC, WIDTH, WIDTH), jnp.bfloat16)] * 2,
        scratch_shapes=[PACKED, BLOCKS],
        compiler_params=PARAMS,
    )(sizes, x, sigma, env)
    part = NSEC // 2
    sent = lax.dynamic_slice_in_dim(renorm, core * part, part, 0)
    positions = lax.axis_size("sweep")
    came = lax.ppermute(sent, "sweep", [(i, i + 1) for i in range(positions - 1)])
    came = lax.all_gather(came, "core", tiled=True)
    next_left = (env.astype(jnp.float32) + came.astype(jnp.float32)).astype(jnp.bfloat16)
    return psi[None], next_left[None]


def solution(mesh):
    positions = mesh.shape["sweep"]
    split = Mesh(
        mesh.devices.reshape(positions, ZH, ZL, X, 2), ("sweep", "zh", "zl", "x", "core")
    )
    ops = ("zh", "zl", "x", "core")
    return jax.shard_map(
        shards,
        mesh=split,
        in_specs=(
            P("sweep", None, None, None),
            P("sweep", ops, None, None, None),
            P("sweep", ops, None, None, None),
            P("sweep", ops, None),
            P("sweep", None),
            P("sweep", None, None, None),
        ),
        out_specs=(P("sweep", None, None, None), P("sweep", None, None, None)),
        check_vma=False,
    )
```

```python
import math

import jax
import jax.numpy as jnp
from jax import lax
from jax.experimental import pallas as pl
from jax.experimental.pallas import tpu as pltpu
from jax.sharding import Mesh, PartitionSpec as P

NSEC = 32
WIDTH = 128
PAIRS = 128
ROWS = 3 * NSEC * WIDTH // 4
HALF = ROWS // 2
TOTAL = NSEC * WIDTH * WIDTH
X, ZL, ZH = 4, 4, 4
NEAR = ZL * X
PIECE = HALF // NEAR
SCALE = 1.0 / math.sqrt(PAIRS)
GROUP = 8
GROUPS = NSEC // GROUP
TAIL = 16

VMEM = pl.BlockSpec(memory_space=pltpu.VMEM)
SMEM = pl.BlockSpec(memory_space=pltpu.SMEM)
HBM = pl.BlockSpec(memory_space=pltpu.HBM)
PACKED = pltpu.VMEM((ROWS + WIDTH, WIDTH), jnp.float32)
BLOCKS = pltpu.VMEM((NSEC, WIDTH, WIDTH), jnp.bfloat16)
SIZES = pltpu.SMEM((1, NSEC), jnp.int32)
PARAMS = pltpu.CompilerParams(vmem_limit_bytes=16 * 1024 * 1024)


def shape(dims, dtype):
    return jax.ShapeDtypeStruct(dims, dtype)


def square_mask(size):
    row = lax.broadcasted_iota(jnp.int32, (WIDTH, WIDTH), 0)
    col = lax.broadcasted_iota(jnp.int32, (WIDTH, WIDTH), 1)
    return (row < size) & (col < size)


def dot(a, b):
    return jnp.dot(a, b, preferred_element_type=jnp.float32)


def fold(value):
    return jnp.sum(value.reshape(WIDTH // 8, 8, WIDTH), axis=0)


def group_copies(pairs, sems):
    return [
        [
            pltpu.make_async_copy(
                source.at[pl.ds(g * GROUP, GROUP)], target.at[pl.ds(g * GROUP, GROUP)], sems.at[g, k]
            )
            for k, (source, target) in enumerate(pairs)
        ]
        for g in range(GROUPS)
    ]


def start_all(copies):
    for group in copies:
        for copy in group:
            copy.start()


def widened(packed, wide):
    wide[pl.ds(0, ROWS), :] = packed[...].astype(jnp.float32)
    wide[pl.ds(ROWS, WIDTH), :] = jnp.zeros((WIDTH, WIDTH), jnp.float32)


def block_of(wide, offset, mask):
    return jnp.where(mask, wide[pl.ds(offset, WIDTH), :], 0.0)


def step_factors(sizes, x_of, sigma, ready):
    zero = jnp.zeros((8, WIDTH), jnp.float32)
    offset, xx, xs, ss = 0, zero, zero, zero
    for g in range(GROUPS):
        ready(g)
        for i in range(g * GROUP, (g + 1) * GROUP):
            mask = square_mask(sizes[0, i])
            x = x_of(i, offset, mask)
            s = block_of(sigma, offset, mask)
            offset = offset + sizes[0, i]
            xx, xs, ss = xx + fold(x * x), xs + fold(x * s), ss + fold(s * s)
    xx, xs, ss = (jnp.sum(v, axis=(0, 1), keepdims=True) for v in (xx, xs, ss))
    rho = xs / xx
    yy = xx + 0.64 * jnp.maximum(ss - rho * xs, 0.0)
    shrink = 1.0 / jnp.sqrt(yy / TOTAL + 1e-06)
    return (1.0 + 0.8 * rho) * shrink, 0.8 * shrink


def run_pairs(meta, sizes, live, xb_of, left, right, env, ready, env_ready, packed, held, mine, other):
    sector = meta[1]

    def body(g, carry):
        offset, at, size_at = carry
        ready(g)
        sums = []
        place = offset
        for j in range(GROUP):
            i = g * GROUP + j
            size = sizes[0, i]
            xb = xb_of(i, place, square_mask(size))
            here = i == sector
            at = jnp.where(here, place, at)
            size_at = jnp.where(here, size, size_at)
            held[i] = xb
            place = place + size
            block = left[i]
            u = live[0, i].astype(jnp.float32) * dot(jnp.concatenate([block, block.T], 0), xb)
            u = u.astype(jnp.bfloat16)
            context = right[i]
            sums.append(
                SCALE
                * dot(
                    jnp.concatenate([u[:WIDTH], u[WIDTH:]], 1),
                    jnp.concatenate([context.T, context], 0),
                )
            )
        for j in range(GROUP):
            packed[pl.ds(offset, WIDTH), :] = sums[j]
            offset = offset + sizes[0, g * GROUP + j]
        return offset, at, size_at

    none = jnp.int32(0)
    _, at, size_at = lax.fori_loop(0, GROUPS, body, (none, none, none))
    env_ready()
    term = 0.25 * dot(env[...], held[sector])
    packed[pl.ds(at, WIDTH), :] += jnp.where(square_mask(size_at), term, 0.0)
    core = meta[0]
    mine[...] = packed[pl.ds(pl.multiple_of(core * HALF, 8), HALF), :]
    other[...] = packed[pl.ds(pl.multiple_of((1 - core) * HALF, 8), HALF), :].astype(jnp.bfloat16)


def scalars_in(sizes_in, live_in, sizes, live, sems):
    copies = [
        pltpu.make_async_copy(sizes_in, sizes, sems.at[0]),
        pltpu.make_async_copy(live_in, live, sems.at[1]),
    ]
    for copy in copies:
        copy.start()
    return copies


def first_kernel(
    meta, sizes_in, live_in, x0_in, left_in, right_in, env_in, mine, other,
    packed, held, x0, left, right, env, sizes, live, sems, own_sems,
):
    small = scalars_in(sizes_in, live_in, sizes, live, own_sems)
    pairs = [(x0_in, x0), (left_in, left), (right_in, right)]
    start_all(group_copies(pairs, sems))
    env_copy = pltpu.make_async_copy(env_in.at[meta[1]], env, own_sems.at[2])
    env_copy.start()
    for copy in small:
        copy.wait()

    def ready(g):
        some = pl.ds(g * GROUP, GROUP)
        for k, (source, target) in enumerate(pairs):
            pltpu.make_async_copy(source.at[some], target.at[some], sems.at[g, k]).wait()

    def xb_of(i, offset, mask):
        x = x0[i]
        return jnp.where(mask, x, jnp.zeros_like(x))

    run_pairs(
        meta, sizes, live, xb_of, left, right, env, ready, env_copy.wait, packed, held, mine, other
    )


def next_kernel(
    meta, sizes_in, live_in, sigma, x0_in, left_in, right_in, env_in, mine, other, factors,
    packed, held, x0, left, right, env, sizes, live, sems, own_sems, x_sems, wide,
):
    small = scalars_in(sizes_in, live_in, sizes, live, own_sems)
    x_copies = group_copies([(x0_in, x0)], x_sems)
    start_all(x_copies)
    pairs = [(left_in, left), (right_in, right)]
    start_all(group_copies(pairs, sems))
    env_copy = pltpu.make_async_copy(env_in.at[meta[1]], env, own_sems.at[2])
    env_copy.start()
    widened(sigma, wide)
    for copy in small:
        copy.wait()

    def x_of(i, offset, mask):
        return jnp.where(mask, x0[i].astype(jnp.float32), 0.0)

    grow, drop = step_factors(sizes, x_of, wide, lambda g: x_copies[g][0].wait())
    factors[0:1, :] = jnp.broadcast_to(grow, (1, WIDTH))
    factors[1:2, :] = jnp.broadcast_to(drop, (1, WIDTH))

    def ready(g):
        some = pl.ds(g * GROUP, GROUP)
        for k, (source, target) in enumerate(pairs):
            pltpu.make_async_copy(source.at[some], target.at[some], sems.at[g, k]).wait()

    def xb_of(i, offset, mask):
        x = grow * x0[i].astype(jnp.float32) - drop * wide[pl.ds(offset, WIDTH), :]
        return jnp.where(mask, x, 0.0).astype(jnp.bfloat16)

    run_pairs(
        meta, sizes, live, xb_of, left, right, env, ready, env_copy.wait, packed, held, mine, other
    )


def last_kernel(
    meta, sizes_in, factors, sigma_before, sigma, x0_in, env_in, psi_out, renorm_out,
    x0, env, psi, sizes, x_sems, env_sems, psi_sems, own_sems, before, wide, packed,
):
    sizes_copy = pltpu.make_async_copy(sizes_in, sizes, own_sems.at[0])
    sizes_copy.start()
    x_copies = group_copies([(x0_in, x0)], x_sems)
    start_all(x_copies)
    env_copies = group_copies([(env_in, env)], env_sems)
    start_all(env_copies)
    psi_copies = group_copies([(psi, psi_out)], psi_sems)
    widened(sigma_before, before)
    widened(sigma, wide)
    grow_before, drop_before = factors[0:1, :], factors[1:2, :]
    sizes_copy.wait()

    def x_of(i, offset, mask):
        x = grow_before * x0[i].astype(jnp.float32) - drop_before * before[pl.ds(offset, WIDTH), :]
        return jnp.where(mask, x, 0.0)

    grow, drop = step_factors(sizes, x_of, wide, lambda g: x_copies[g][0].wait())
    offset = 0
    for g in range(GROUPS):
        env_copies[g][0].wait()
        some = range(g * GROUP, (g + 1) * GROUP)
        blocks = []
        place = offset
        for i in some:
            mask = square_mask(sizes[0, i])
            new = grow * x_of(i, place, mask) - drop * block_of(wide, place, mask)
            new = new.astype(jnp.bfloat16)
            psi[i] = new
            place = place + sizes[0, i]
            applied = dot(env[i], new).astype(jnp.bfloat16)
            blocks.append(dot(new.T, applied) / math.sqrt(WIDTH))
        psi_copies[g][0].start()
        for i, block in zip(some, blocks):
            packed[pl.ds(offset, WIDTH), :] = block
            offset = offset + sizes[0, i]
    core = meta[0]
    renorm_out[pl.ds(0, HALF), :] = packed[
        pl.ds(pl.multiple_of(core * HALF, 8), HALF), :
    ].astype(jnp.bfloat16)
    lane = lax.broadcasted_iota(jnp.int32, (TAIL, WIDTH), 1)
    row = jnp.zeros((TAIL, WIDTH), jnp.int32)
    for i in range(NSEC):
        row = jnp.where(lane == i, sizes[0, i], row)
    renorm_out[pl.ds(HALF, TAIL), :] = row.astype(jnp.float32).astype(jnp.bfloat16)
    for copies in psi_copies:
        copies[0].wait()


def shift_kernel(came, env, out, wide, result, numbers, sizes, sems, own_sem):
    numbers[...] = came[pl.ds(HALF, 8), :].astype(jnp.float32).astype(jnp.int32)
    sizes_copy = pltpu.make_async_copy(numbers, sizes, own_sem.at[0])
    sizes_copy.start()
    wide[pl.ds(0, HALF), :] = came[pl.ds(0, HALF), :].astype(jnp.float32)
    wide[pl.ds(HALF, HALF), :] = came[pl.ds(HALF + TAIL, HALF), :].astype(jnp.float32)
    wide[pl.ds(ROWS, WIDTH), :] = jnp.zeros((WIDTH, WIDTH), jnp.float32)
    sizes_copy.wait()
    copies = group_copies([(result, out)], sems)
    offset = 0
    for g in range(GROUPS):
        for i in range(g * GROUP, (g + 1) * GROUP):
            block = block_of(wide, offset, square_mask(sizes[0, i]))
            result[i] = (env[i].astype(jnp.float32) + block).astype(jnp.bfloat16)
            offset = offset + sizes[0, i]
        copies[g][0].start()
    for group in copies:
        group[0].wait()


def sum_kernel(parts, out):
    total = jnp.sum(parts[...].astype(jnp.float32), axis=0).astype(jnp.bfloat16)
    for k in range(out.shape[0]):
        out[k] = total


def summed(parts, copies):
    return pl.pallas_call(
        sum_kernel,
        in_specs=[VMEM],
        out_specs=VMEM,
        out_shape=shape((copies,) + parts.shape[1:], parts.dtype),
    )(parts)


def exchange(value, axes):
    return lax.all_to_all(value, axes, 0, 0)


def all_summed(mine, other):
    came = lax.ppermute(other, "core", [(0, 1), (1, 0)])
    chip = (mine + came.astype(jnp.float32)).astype(jnp.bfloat16).reshape(NEAR, PIECE, WIDTH)
    near = summed(exchange(chip, ("zl", "x")), ZH)
    far = summed(exchange(near, "zh"), NEAR)
    half = exchange(far, ("zl", "x"))
    return lax.all_gather(half.reshape(HALF, WIDTH), "core", tiled=True)


def dma(*dims):
    return pltpu.SemaphoreType.DMA(dims)


def shards(initial_trial_state, left_ops, right_ops, pair_sectors, sector_size, left_env):
    x0 = initial_trial_state[0]
    left = left_ops[0, 0]
    right = right_ops[0, 0]
    live = pair_sectors[0]
    sizes = sector_size
    env = left_env[0]
    core = lax.axis_index("core")
    sector = lax.axis_index(("zh", "zl", "x", "core")) // (PAIRS // NSEC)
    meta = jnp.stack([core, sector]).astype(jnp.int32)

    sums = [shape((HALF, WIDTH), jnp.float32), shape((HALF, WIDTH), jnp.bfloat16)]
    scratch = [PACKED, BLOCKS, BLOCKS, BLOCKS, BLOCKS, pltpu.VMEM((WIDTH, WIDTH), jnp.bfloat16)]
    scratch += [SIZES, SIZES]
    mine, other = pl.pallas_call(
        first_kernel,
        in_specs=[SMEM] + [HBM] * 6,
        out_specs=[VMEM] * 2,
        out_shape=sums,
        scratch_shapes=scratch + [dma(GROUPS, 3), dma(3)],
        compiler_params=PARAMS,
    )(meta, sizes, live, x0, left, right, env)
    before = all_summed(mine, other)
    mine, other, factors = pl.pallas_call(
        next_kernel,
        in_specs=[SMEM, HBM, HBM, VMEM] + [HBM] * 4,
        out_specs=[VMEM] * 3,
        out_shape=sums + [shape((2, WIDTH), jnp.float32)],
        scratch_shapes=scratch + [dma(GROUPS, 2), dma(3), dma(GROUPS, 1), PACKED],
        compiler_params=PARAMS,
    )(meta, sizes, live, before, x0, left, right, env)
    sigma = all_summed(mine, other)
    psi, renorm = pl.pallas_call(
        last_kernel,
        in_specs=[SMEM, HBM] + [VMEM] * 3 + [HBM] * 2,
        out_specs=[HBM, VMEM],
        out_shape=[
            shape((NSEC, WIDTH, WIDTH), jnp.bfloat16),
            shape((HALF + TAIL, WIDTH), jnp.bfloat16),
        ],
        scratch_shapes=[BLOCKS, BLOCKS, BLOCKS, SIZES]
        + [dma(GROUPS, 1), dma(GROUPS, 1), dma(GROUPS, 1), dma(1), PACKED, PACKED, PACKED],
        compiler_params=PARAMS,
    )(meta, sizes, factors, before, sigma, x0, env)
    positions = lax.axis_size("sweep")
    came = lax.ppermute(renorm, "sweep", [(i, i + 1) for i in range(positions - 1)])
    came = lax.all_gather(came, "core", tiled=True)
    next_left = pl.pallas_call(
        shift_kernel,
        in_specs=[VMEM] * 2,
        out_specs=HBM,
        out_shape=shape((NSEC, WIDTH, WIDTH), jnp.bfloat16),
        scratch_shapes=[
            PACKED,
            BLOCKS,
            pltpu.VMEM((8, WIDTH), jnp.int32),
            pltpu.SMEM((8, WIDTH), jnp.int32),
            dma(GROUPS, 1),
            dma(1),
        ],
        compiler_params=PARAMS,
    )(came, env)
    return psi[None], next_left[None]


def solution(mesh):
    positions = mesh.shape["sweep"]
    split = Mesh(
        mesh.devices.reshape(positions, ZH, ZL, X, 2), ("sweep", "zh", "zl", "x", "core")
    )
    ops = ("zh", "zl", "x", "core")
    return jax.shard_map(
        shards,
        mesh=split,
        in_specs=(
            P("sweep", None, None, None),
            P("sweep", ops, None, None, None),
            P("sweep", ops, None, None, None),
            P("sweep", ops, None),
            P("sweep", None),
            P("sweep", None, None, None),
        ),
        out_specs=(P("sweep", None, None, None), P("sweep", None, None, None)),
        check_vma=False,
    )
```

```python
import math

import jax
import jax.numpy as jnp
from jax import lax
from jax.experimental import pallas as pl
from jax.experimental.pallas import tpu as pltpu
from jax.sharding import Mesh, PartitionSpec as P

NSEC = 32
WIDTH = 128
PAIRS = 128
ROWS = 3 * NSEC * WIDTH // 4
HALF = ROWS // 2
TOTAL = NSEC * WIDTH * WIDTH
X, ZL, ZH = 4, 4, 4
NEAR = ZL * X
PIECE = HALF // NEAR
SCALE = 1.0 / math.sqrt(PAIRS)
GROUP = 8
GROUPS = NSEC // GROUP
TAIL = 16

VMEM = pl.BlockSpec(memory_space=pltpu.VMEM)
SMEM = pl.BlockSpec(memory_space=pltpu.SMEM)
HBM = pl.BlockSpec(memory_space=pltpu.HBM)
PACKED = pltpu.VMEM((ROWS + WIDTH, WIDTH), jnp.float32)
BLOCKS = pltpu.VMEM((NSEC, WIDTH, WIDTH), jnp.bfloat16)
SIZES = pltpu.SMEM((1, NSEC), jnp.int32)


def limit(mib):
    return pltpu.CompilerParams(vmem_limit_bytes=mib * 1024 * 1024)


def shape(dims, dtype):
    return jax.ShapeDtypeStruct(dims, dtype)


def square_mask(size):
    row = lax.broadcasted_iota(jnp.int32, (WIDTH, WIDTH), 0)
    col = lax.broadcasted_iota(jnp.int32, (WIDTH, WIDTH), 1)
    return (row < size) & (col < size)


def dot(a, b):
    return jnp.dot(a, b, preferred_element_type=jnp.float32)


def fold(value):
    return jnp.sum(value.reshape(WIDTH // 8, 8, WIDTH), axis=0)


def group_copies(pairs, sems):
    return [
        [
            pltpu.make_async_copy(
                source.at[pl.ds(g * GROUP, GROUP)], target.at[pl.ds(g * GROUP, GROUP)], sems.at[g, k]
            )
            for k, (source, target) in enumerate(pairs)
        ]
        for g in range(GROUPS)
    ]


def start_all(copies):
    for group in copies:
        for copy in group:
            copy.start()


def widened(packed, wide):
    wide[pl.ds(0, ROWS), :] = packed[...].astype(jnp.float32)
    wide[pl.ds(ROWS, WIDTH), :] = jnp.zeros((WIDTH, WIDTH), jnp.float32)


def block_of(wide, offset, mask):
    return jnp.where(mask, wide[pl.ds(offset, WIDTH), :], 0.0)


def step_factors(sizes, x_of, sigma, ready):
    zero = jnp.zeros((8, WIDTH), jnp.float32)
    offset, xx, xs, ss = 0, zero, zero, zero
    for g in range(GROUPS):
        ready(g)
        for i in range(g * GROUP, (g + 1) * GROUP):
            mask = square_mask(sizes[0, i])
            x = x_of(i, offset, mask)
            s = block_of(sigma, offset, mask)
            offset = offset + sizes[0, i]
            xx, xs, ss = xx + fold(x * x), xs + fold(x * s), ss + fold(s * s)
    xx, xs, ss = (jnp.sum(v, axis=(0, 1), keepdims=True) for v in (xx, xs, ss))
    rho = xs / xx
    yy = xx + 0.64 * jnp.maximum(ss - rho * xs, 0.0)
    shrink = 1.0 / jnp.sqrt(yy / TOTAL + 1e-06)
    return (1.0 + 0.8 * rho) * shrink, 0.8 * shrink


def run_pairs(meta, sizes, live, xb_of, left, right, env, ready, env_ready, packed, held, mine, other):
    sector = meta[1]

    def body(g, carry):
        offset, at, size_at = carry
        ready(g)
        sums = []
        place = offset
        for j in range(GROUP):
            i = g * GROUP + j
            size = sizes[0, i]
            xb = xb_of(i, place, square_mask(size))
            here = i == sector
            at = jnp.where(here, place, at)
            size_at = jnp.where(here, size, size_at)
            held[i] = xb
            place = place + size
            block = left[i]
            u = live[0, i].astype(jnp.float32) * dot(jnp.concatenate([block, block.T], 0), xb)
            u = u.astype(jnp.bfloat16)
            context = right[i]
            sums.append(
                SCALE
                * dot(
                    jnp.concatenate([u[:WIDTH], u[WIDTH:]], 1),
                    jnp.concatenate([context.T, context], 0),
                )
            )
        for j in range(GROUP):
            packed[pl.ds(offset, WIDTH), :] = sums[j]
            offset = offset + sizes[0, g * GROUP + j]
        return offset, at, size_at

    none = jnp.int32(0)
    _, at, size_at = lax.fori_loop(0, GROUPS, body, (none, none, none))
    env_ready()
    term = 0.25 * dot(env[...], held[sector])
    packed[pl.ds(at, WIDTH), :] += jnp.where(square_mask(size_at), term, 0.0)
    core = meta[0]
    mine[...] = packed[pl.ds(pl.multiple_of(core * HALF, 8), HALF), :]
    other[...] = packed[pl.ds(pl.multiple_of((1 - core) * HALF, 8), HALF), :].astype(jnp.bfloat16)


def scalars_in(sizes_in, live_in, sizes, live, sems):
    copies = [
        pltpu.make_async_copy(sizes_in, sizes, sems.at[0]),
        pltpu.make_async_copy(live_in, live, sems.at[1]),
    ]
    for copy in copies:
        copy.start()
    return copies


def first_kernel(
    meta, sizes_in, live_in, x0_in, left_in, right_in, env_in, mine, other,
    packed, held, x0, left, right, env, sizes, live, sems, own_sems,
):
    small = scalars_in(sizes_in, live_in, sizes, live, own_sems)
    pairs = [(x0_in, x0), (left_in, left), (right_in, right)]
    start_all(group_copies(pairs, sems))
    env_copy = pltpu.make_async_copy(env_in.at[meta[1]], env, own_sems.at[2])
    env_copy.start()
    for copy in small:
        copy.wait()

    def ready(g):
        some = pl.ds(g * GROUP, GROUP)
        for k, (source, target) in enumerate(pairs):
            pltpu.make_async_copy(source.at[some], target.at[some], sems.at[g, k]).wait()

    def xb_of(i, offset, mask):
        x = x0[i]
        return jnp.where(mask, x, jnp.zeros_like(x))

    run_pairs(
        meta, sizes, live, xb_of, left, right, env, ready, env_copy.wait, packed, held, mine, other
    )


def next_kernel(
    meta, sizes_in, live_in, sigma, x0_in, left_in, right_in, env_in, mine, other, factors,
    packed, held, x0, left, right, env, sizes, live, sems, own_sems, x_sems, wide,
):
    small = scalars_in(sizes_in, live_in, sizes, live, own_sems)
    x_copies = group_copies([(x0_in, x0)], x_sems)
    start_all(x_copies)
    pairs = [(left_in, left), (right_in, right)]
    start_all(group_copies(pairs, sems))
    env_copy = pltpu.make_async_copy(env_in.at[meta[1]], env, own_sems.at[2])
    env_copy.start()
    widened(sigma, wide)
    for copy in small:
        copy.wait()

    def x_of(i, offset, mask):
        return jnp.where(mask, x0[i].astype(jnp.float32), 0.0)

    grow, drop = step_factors(sizes, x_of, wide, lambda g: x_copies[g][0].wait())
    factors[0:1, :] = jnp.broadcast_to(grow, (1, WIDTH))
    factors[1:2, :] = jnp.broadcast_to(drop, (1, WIDTH))

    def ready(g):
        some = pl.ds(g * GROUP, GROUP)
        for k, (source, target) in enumerate(pairs):
            pltpu.make_async_copy(source.at[some], target.at[some], sems.at[g, k]).wait()

    def xb_of(i, offset, mask):
        x = grow * x0[i].astype(jnp.float32) - drop * wide[pl.ds(offset, WIDTH), :]
        return jnp.where(mask, x, 0.0).astype(jnp.bfloat16)

    run_pairs(
        meta, sizes, live, xb_of, left, right, env, ready, env_copy.wait, packed, held, mine, other
    )


def last_kernel(
    meta, sizes_in, factors, sigma_before, sigma, x0_in, env_in, psi_out, renorm_out,
    x0, env, psi, sizes, x_sems, env_sems, psi_sems, own_sems, before, wide, packed,
):
    sizes_copy = pltpu.make_async_copy(sizes_in, sizes, own_sems.at[0])
    sizes_copy.start()
    x_copies = group_copies([(x0_in, x0)], x_sems)
    start_all(x_copies)
    env_copies = group_copies([(env_in, env)], env_sems)
    start_all(env_copies)
    psi_copies = group_copies([(psi, psi_out)], psi_sems)
    widened(sigma_before, before)
    widened(sigma, wide)
    grow_before, drop_before = factors[0:1, :], factors[1:2, :]
    sizes_copy.wait()

    def x_of(i, offset, mask):
        x = grow_before * x0[i].astype(jnp.float32) - drop_before * before[pl.ds(offset, WIDTH), :]
        return jnp.where(mask, x, 0.0)

    grow, drop = step_factors(sizes, x_of, wide, lambda g: x_copies[g][0].wait())
    offset = 0
    for g in range(GROUPS):
        env_copies[g][0].wait()
        some = range(g * GROUP, (g + 1) * GROUP)
        blocks = []
        place = offset
        for i in some:
            mask = square_mask(sizes[0, i])
            new = grow * x_of(i, place, mask) - drop * block_of(wide, place, mask)
            new = new.astype(jnp.bfloat16)
            psi[i] = new
            place = place + sizes[0, i]
            applied = dot(env[i], new).astype(jnp.bfloat16)
            blocks.append(dot(new.T, applied) / math.sqrt(WIDTH))
        psi_copies[g][0].start()
        for i, block in zip(some, blocks):
            packed[pl.ds(offset, WIDTH), :] = block
            offset = offset + sizes[0, i]
    core = meta[0]
    renorm_out[pl.ds(0, HALF), :] = packed[
        pl.ds(pl.multiple_of(core * HALF, 8), HALF), :
    ].astype(jnp.bfloat16)
    lane = lax.broadcasted_iota(jnp.int32, (TAIL, WIDTH), 1)
    row = jnp.zeros((TAIL, WIDTH), jnp.int32)
    for i in range(NSEC):
        row = jnp.where(lane == i, sizes[0, i], row)
    renorm_out[pl.ds(HALF, TAIL), :] = row.astype(jnp.float32).astype(jnp.bfloat16)
    for copies in psi_copies:
        copies[0].wait()


def shift_kernel(came, env, out, wide, result, numbers, sizes, sems, own_sem):
    numbers[...] = came[pl.ds(HALF, 8), :].astype(jnp.float32).astype(jnp.int32)
    sizes_copy = pltpu.make_async_copy(numbers, sizes, own_sem.at[0])
    sizes_copy.start()
    wide[pl.ds(0, HALF), :] = came[pl.ds(0, HALF), :].astype(jnp.float32)
    wide[pl.ds(HALF, HALF), :] = came[pl.ds(HALF + TAIL, HALF), :].astype(jnp.float32)
    wide[pl.ds(ROWS, WIDTH), :] = jnp.zeros((WIDTH, WIDTH), jnp.float32)
    sizes_copy.wait()
    copies = group_copies([(result, out)], sems)
    offset = 0
    for g in range(GROUPS):
        for i in range(g * GROUP, (g + 1) * GROUP):
            block = block_of(wide, offset, square_mask(sizes[0, i]))
            result[i] = (env[i].astype(jnp.float32) + block).astype(jnp.bfloat16)
            offset = offset + sizes[0, i]
        copies[g][0].start()
    for group in copies:
        group[0].wait()


def sum_kernel(parts, out):
    total = jnp.sum(parts[...].astype(jnp.float32), axis=0).astype(jnp.bfloat16)
    for k in range(out.shape[0]):
        out[k] = total


def summed(parts, copies):
    return pl.pallas_call(
        sum_kernel,
        in_specs=[VMEM],
        out_specs=VMEM,
        out_shape=shape((copies,) + parts.shape[1:], parts.dtype),
        compiler_params=limit(4),
    )(parts)


def exchange(value, axes):
    return lax.all_to_all(value, axes, 0, 0)


def all_summed(mine, other):
    came = lax.ppermute(other, "core", [(0, 1), (1, 0)])
    chip = (mine + came.astype(jnp.float32)).astype(jnp.bfloat16).reshape(NEAR, PIECE, WIDTH)
    near = summed(exchange(chip, ("zl", "x")), ZH)
    far = summed(exchange(near, "zh"), NEAR)
    half = exchange(far, ("zl", "x"))
    return lax.all_gather(half.reshape(HALF, WIDTH), "core", tiled=True)


def dma(*dims):
    return pltpu.SemaphoreType.DMA(dims)


def shards(initial_trial_state, left_ops, right_ops, pair_sectors, sector_size, left_env):
    x0 = initial_trial_state[0]
    left = left_ops[0, 0]
    right = right_ops[0, 0]
    live = pair_sectors[0]
    sizes = sector_size
    env = left_env[0]
    core = lax.axis_index("core")
    sector = lax.axis_index(("zh", "zl", "x", "core")) // (PAIRS // NSEC)
    meta = jnp.stack([core, sector]).astype(jnp.int32)

    sums = [shape((HALF, WIDTH), jnp.float32), shape((HALF, WIDTH), jnp.bfloat16)]
    scratch = [PACKED, BLOCKS, BLOCKS, BLOCKS, BLOCKS, pltpu.VMEM((WIDTH, WIDTH), jnp.bfloat16)]
    scratch += [SIZES, SIZES]
    mine, other = pl.pallas_call(
        first_kernel,
        in_specs=[SMEM] + [HBM] * 6,
        out_specs=[VMEM] * 2,
        out_shape=sums,
        scratch_shapes=scratch + [dma(GROUPS, 3), dma(3)],
        compiler_params=limit(52),
    )(meta, sizes, live, x0, left, right, env)
    before = all_summed(mine, other)
    mine, other, factors = pl.pallas_call(
        next_kernel,
        in_specs=[SMEM, HBM, HBM, VMEM] + [HBM] * 4,
        out_specs=[VMEM] * 3,
        out_shape=sums + [shape((2, WIDTH), jnp.float32)],
        scratch_shapes=scratch + [dma(GROUPS, 2), dma(3), dma(GROUPS, 1), PACKED],
        compiler_params=limit(12),
    )(meta, sizes, live, before, x0, left, right, env)
    sigma = all_summed(mine, other)
    psi, renorm = pl.pallas_call(
        last_kernel,
        in_specs=[SMEM, HBM] + [VMEM] * 3 + [HBM] * 2,
        out_specs=[HBM, VMEM],
        out_shape=[
            shape((NSEC, WIDTH, WIDTH), jnp.bfloat16),
            shape((HALF + TAIL, WIDTH), jnp.bfloat16),
        ],
        scratch_shapes=[BLOCKS, BLOCKS, BLOCKS, SIZES]
        + [dma(GROUPS, 1), dma(GROUPS, 1), dma(GROUPS, 1), dma(1), PACKED, PACKED, PACKED],
        compiler_params=limit(12),
    )(meta, sizes, factors, before, sigma, x0, env)
    positions = lax.axis_size("sweep")
    came = lax.ppermute(renorm, "sweep", [(i, i + 1) for i in range(positions - 1)])
    came = lax.all_gather(came, "core", tiled=True)
    next_left = pl.pallas_call(
        shift_kernel,
        in_specs=[VMEM] * 2,
        out_specs=HBM,
        out_shape=shape((NSEC, WIDTH, WIDTH), jnp.bfloat16),
        scratch_shapes=[
            PACKED,
            BLOCKS,
            pltpu.VMEM((8, WIDTH), jnp.int32),
            pltpu.SMEM((8, WIDTH), jnp.int32),
            dma(GROUPS, 1),
            dma(1),
        ],
        compiler_params=limit(8),
    )(came, env)
    return psi[None], next_left[None]


def solution(mesh):
    positions = mesh.shape["sweep"]
    split = Mesh(
        mesh.devices.reshape(positions, ZH, ZL, X, 2), ("sweep", "zh", "zl", "x", "core")
    )
    ops = ("zh", "zl", "x", "core")
    return jax.shard_map(
        shards,
        mesh=split,
        in_specs=(
            P("sweep", None, None, None),
            P("sweep", ops, None, None, None),
            P("sweep", ops, None, None, None),
            P("sweep", ops, None),
            P("sweep", None),
            P("sweep", None, None, None),
        ),
        out_specs=(P("sweep", None, None, None), P("sweep", None, None, None)),
        check_vma=False,
    )
```

```python
import math

import jax
import jax.numpy as jnp
from jax import lax
from jax.experimental import pallas as pl
from jax.experimental.pallas import tpu as pltpu
from jax.sharding import Mesh, PartitionSpec as P

NSEC = 32
WIDTH = 128
PAIRS = 128
ROWS = 3 * NSEC * WIDTH // 4
HALF = ROWS // 2
TOTAL = NSEC * WIDTH * WIDTH
X, ZL, ZH = 4, 4, 4
NEAR = ZL * X
PIECE = HALF // NEAR
SCALE = 1.0 / math.sqrt(PAIRS)
GROUP = 8
GROUPS = NSEC // GROUP
TAIL = 16
CHUNK = 256

VMEM = pl.BlockSpec(memory_space=pltpu.VMEM)
SMEM = pl.BlockSpec(memory_space=pltpu.SMEM)
HBM = pl.BlockSpec(memory_space=pltpu.HBM)
PACKED = pltpu.VMEM((ROWS + WIDTH, WIDTH), jnp.float32)
BLOCKS = pltpu.VMEM((NSEC, WIDTH, WIDTH), jnp.bfloat16)


def limit(mib):
    return pltpu.CompilerParams(vmem_limit_bytes=mib * 1024 * 1024)


def shape(dims, dtype):
    return jax.ShapeDtypeStruct(dims, dtype)


def square_mask(size):
    row = lax.broadcasted_iota(jnp.int32, (WIDTH, WIDTH), 0)
    col = lax.broadcasted_iota(jnp.int32, (WIDTH, WIDTH), 1)
    return (row < size) & (col < size)


def dot(a, b):
    return jnp.dot(a, b, preferred_element_type=jnp.float32)


def group_copies(pairs, sems):
    return [
        [
            pltpu.make_async_copy(
                source.at[pl.ds(g * GROUP, GROUP)], target.at[pl.ds(g * GROUP, GROUP)], sems.at[g, k]
            )
            for k, (source, target) in enumerate(pairs)
        ]
        for g in range(GROUPS)
    ]


def start_all(copies):
    for group in copies:
        for copy in group:
            copy.start()


def flat_sums(pairs):
    totals = None
    for start in range(0, ROWS, CHUNK):
        parts = [
            jnp.sum((p * q).reshape(CHUNK // 8, 8, WIDTH), axis=0)
            for p, q in pairs(pl.ds(start, CHUNK))
        ]
        totals = parts if totals is None else [t + p for t, p in zip(totals, parts)]
    return [jnp.sum(t, axis=(0, 1), keepdims=True) for t in totals]


def step_factors(x_of, sigma):
    def products(rows):
        x, s = x_of(rows), sigma[rows, :].astype(jnp.float32)
        return [(x, x), (x, s), (s, s)]

    xx, xs, ss = flat_sums(products)
    rho = xs / xx
    yy = xx + 0.64 * jnp.maximum(ss - rho * xs, 0.0)
    shrink = 1.0 / jnp.sqrt(yy / TOTAL + 1e-06)
    return (1.0 + 0.8 * rho) * shrink, 0.8 * shrink


def size_of(meta, i):
    return meta[2 + i]


def rows_below(size):
    return lax.broadcasted_iota(jnp.int32, (WIDTH, WIDTH), 0) < size


def run_pairs(meta, xb_of, left, right, env, ready, env_ready, packed, mine, other):
    sector = meta[1]
    column = lax.broadcasted_iota(jnp.int32, (WIDTH, WIDTH), 1)

    def body(g, carry):
        offset, at = carry
        ready(g)
        sums = []
        place = offset
        for j in range(GROUP):
            i = g * GROUP + j
            xb = xb_of(i, place)
            at = jnp.where(i == sector, place, at)
            place = place + size_of(meta, i)
            block = left[i]
            live = meta[2 + NSEC + i].astype(jnp.float32)
            u = live * dot(jnp.concatenate([block, block.T], 0), xb)
            u = u.astype(jnp.bfloat16)
            context = right[i]
            total = SCALE * dot(
                jnp.concatenate([u[:WIDTH], u[WIDTH:]], 1),
                jnp.concatenate([context.T, context], 0),
            )
            sums.append(jnp.where(column < size_of(meta, i), total, 0.0))
        for j in range(GROUP):
            packed[pl.ds(offset, WIDTH), :] = sums[j]
            offset = offset + size_of(meta, g * GROUP + j)
        return offset, at

    _, at = lax.fori_loop(0, GROUPS, body, (jnp.int32(0), jnp.int32(0)))
    env_ready()
    term = 0.25 * dot(env[...], xb_of(sector, at, keep=False))
    packed[pl.ds(at, WIDTH), :] += jnp.where(square_mask(size_of(meta, sector)), term, 0.0)
    core = meta[0]
    mine[...] = packed[pl.ds(pl.multiple_of(core * HALF, 8), HALF), :]
    other[...] = packed[pl.ds(pl.multiple_of((1 - core) * HALF, 8), HALF), :].astype(jnp.bfloat16)


def first_kernel(
    meta, x0_in, left_in, right_in, env_in, mine, other, x_out,
    packed, x0, left, right, env, sems, env_sem, x_packed,
):
    pairs = [(x0_in, x0), (left_in, left), (right_in, right)]
    start_all(group_copies(pairs, sems))
    env_copy = pltpu.make_async_copy(env_in.at[meta[1]], env, env_sem.at[0])
    env_copy.start()

    def ready(g):
        some = pl.ds(g * GROUP, GROUP)
        for k, (source, target) in enumerate(pairs):
            pltpu.make_async_copy(source.at[some], target.at[some], sems.at[g, k]).wait()

    def xb_of(i, offset, keep=True):
        x = jnp.where(square_mask(size_of(meta, i)), x0[i].astype(jnp.float32), 0.0)
        if keep:
            x_packed[pl.ds(offset, WIDTH), :] = x
        return x.astype(jnp.bfloat16)

    run_pairs(meta, xb_of, left, right, env, ready, env_copy.wait, packed, mine, other)
    x_out[...] = x_packed[pl.ds(0, ROWS), :].astype(jnp.bfloat16)


def next_kernel(
    meta, sigma, x0, left, right, env_in, mine, other, factors, packed, env, env_sem, wide
):
    env_copy = pltpu.make_async_copy(env_in.at[meta[1]], env, env_sem.at[0])
    env_copy.start()

    def x_of(rows):
        return x0[rows, :].astype(jnp.float32)

    grow, drop = step_factors(x_of, sigma)
    factors[0:1, :] = jnp.broadcast_to(grow, (1, WIDTH))
    factors[1:2, :] = jnp.broadcast_to(drop, (1, WIDTH))
    wide[pl.ds(0, ROWS), :] = grow * x_of(pl.ds(0, ROWS)) - drop * sigma[...].astype(jnp.float32)

    def xb_of(i, offset, keep=True):
        mask = rows_below(size_of(meta, i))
        return jnp.where(mask, wide[pl.ds(offset, WIDTH), :], 0.0).astype(jnp.bfloat16)

    run_pairs(meta, xb_of, left, right, env, lambda g: None, env_copy.wait, packed, mine, other)


def renorm_kernel(
    meta, factors, sigma_before, sigma, x0, env, psi_out, renorm_out, wide, packed
):
    grow_before, drop_before = factors[0:1, :], factors[1:2, :]

    def x_of(rows):
        return grow_before * x0[rows, :].astype(jnp.float32) - drop_before * sigma_before[
            rows, :
        ].astype(jnp.float32)

    grow, drop = step_factors(x_of, sigma)
    psi = grow * x_of(pl.ds(0, ROWS)) - drop * sigma[...].astype(jnp.float32)
    psi = psi.astype(jnp.bfloat16)
    psi_out[...] = psi
    wide[pl.ds(0, ROWS), :] = psi.astype(jnp.float32)
    low = pl.multiple_of(meta[0] * HALF, 8)
    high = low + HALF
    offset = 0
    for g in range(GROUPS):
        places = [offset]
        for i in range(g * GROUP, (g + 1) * GROUP):
            places.append(places[-1] + size_of(meta, i))
        offset = places[-1]

        @pl.when((places[0] < high) & (offset > low))
        def _():
            blocks = []
            for i, place in zip(range(g * GROUP, (g + 1) * GROUP), places):
                block = jnp.where(rows_below(size_of(meta, i)), wide[pl.ds(place, WIDTH), :], 0.0)
                block = block.astype(jnp.bfloat16)
                applied = dot(env[i], block).astype(jnp.bfloat16)
                blocks.append(dot(block.T, applied) / math.sqrt(WIDTH))
            for place, block in zip(places, blocks):
                packed[pl.ds(place, WIDTH), :] = block

    renorm_out[pl.ds(0, HALF), :] = packed[pl.ds(low, HALF), :].astype(jnp.bfloat16)
    lane = lax.broadcasted_iota(jnp.int32, (TAIL, WIDTH), 1)
    row = jnp.zeros((TAIL, WIDTH), jnp.int32)
    for i in range(NSEC):
        row = jnp.where(lane == i, size_of(meta, i), row)
    renorm_out[pl.ds(HALF, TAIL), :] = row.astype(jnp.float32).astype(jnp.bfloat16)


def unpack(size_at, wide, result, out, sems, finish):
    copies = group_copies([(result, out)], sems)
    offset = 0
    for g in range(GROUPS):
        for i in range(g * GROUP, (g + 1) * GROUP):
            size = size_at(i)
            block = jnp.where(rows_below(size), wide[pl.ds(offset, WIDTH), :], 0.0)
            result[i] = finish(i, block).astype(jnp.bfloat16)
            offset = offset + size
        copies[g][0].start()
    for group in copies:
        group[0].wait()


def psi_kernel(meta, psi, out, wide, result, sems):
    wide[pl.ds(0, ROWS), :] = psi[...].astype(jnp.float32)
    unpack(lambda i: size_of(meta, i), wide, result, out, sems, lambda i, block: block)


def shift_kernel(came, env, out, wide, result, numbers, sizes, sems, own_sem):
    numbers[...] = came[pl.ds(HALF, 8), :].astype(jnp.float32).astype(jnp.int32)
    sizes_copy = pltpu.make_async_copy(numbers, sizes, own_sem.at[0])
    sizes_copy.start()
    wide[pl.ds(0, HALF), :] = came[pl.ds(0, HALF), :].astype(jnp.float32)
    wide[pl.ds(HALF, HALF), :] = came[pl.ds(HALF + TAIL, HALF), :].astype(jnp.float32)
    sizes_copy.wait()
    unpack(
        lambda i: sizes[0, i],
        wide,
        result,
        out,
        sems,
        lambda i, block: env[i].astype(jnp.float32) + block,
    )


def sum_kernel(parts, out):
    total = jnp.sum(parts[...].astype(jnp.float32), axis=0).astype(jnp.bfloat16)
    for k in range(out.shape[0]):
        out[k] = total


def summed(parts, copies):
    return pl.pallas_call(
        sum_kernel,
        in_specs=[VMEM],
        out_specs=VMEM,
        out_shape=shape((copies,) + parts.shape[1:], parts.dtype),
        compiler_params=limit(4),
    )(parts)


def exchange(value, axes):
    return lax.all_to_all(value, axes, 0, 0)


def all_summed(mine, other):
    came = lax.ppermute(other, "core", [(0, 1), (1, 0)])
    chip = (mine + came.astype(jnp.float32)).astype(jnp.bfloat16).reshape(NEAR, PIECE, WIDTH)
    near = summed(exchange(chip, ("zl", "x")), ZH)
    far = summed(exchange(near, "zh"), NEAR)
    half = exchange(far, ("zl", "x"))
    return lax.all_gather(half.reshape(HALF, WIDTH), "core", tiled=True)


def dma(*dims):
    return pltpu.SemaphoreType.DMA(dims)


def shards(initial_trial_state, left_ops, right_ops, pair_sectors, sector_size, left_env):
    x0 = initial_trial_state[0]
    left = left_ops[0, 0]
    right = right_ops[0, 0]
    env = left_env[0]
    core = lax.axis_index("core")
    sector = lax.axis_index(("zh", "zl", "x", "core")) // (PAIRS // NSEC)
    own = jnp.stack([core, sector]).astype(jnp.int32)
    meta = jnp.concatenate([own, sector_size[0], pair_sectors[0, 0]])

    sums = [shape((HALF, WIDTH), jnp.float32), shape((HALF, WIDTH), jnp.bfloat16)]
    rows = shape((ROWS, WIDTH), jnp.bfloat16)
    blocks = shape((NSEC, WIDTH, WIDTH), jnp.bfloat16)
    env_scratch = [pltpu.VMEM((WIDTH, WIDTH), jnp.bfloat16)]
    mine, other, x0 = pl.pallas_call(
        first_kernel,
        in_specs=[SMEM] + [HBM] * 4,
        out_specs=[VMEM] * 3,
        out_shape=sums + [rows],
        scratch_shapes=[PACKED, BLOCKS, BLOCKS, BLOCKS]
        + env_scratch
        + [dma(GROUPS, 3), dma(1), PACKED],
        compiler_params=limit(52),
    )(meta, x0, left, right, env)
    before = all_summed(mine, other)
    mine, other, factors = pl.pallas_call(
        next_kernel,
        in_specs=[SMEM] + [VMEM] * 4 + [HBM],
        out_specs=[VMEM] * 3,
        out_shape=sums + [shape((2, WIDTH), jnp.float32)],
        scratch_shapes=[PACKED] + env_scratch + [dma(1), PACKED],
        compiler_params=limit(12),
    )(meta, before, x0, left, right, env)
    sigma = all_summed(mine, other)
    psi, renorm = pl.pallas_call(
        renorm_kernel,
        in_specs=[SMEM] + [VMEM] * 5,
        out_specs=[VMEM] * 2,
        out_shape=[rows, shape((HALF + TAIL, WIDTH), jnp.bfloat16)],
        scratch_shapes=[PACKED, PACKED],
        compiler_params=limit(12),
    )(meta, factors, before, sigma, x0, env)
    positions = lax.axis_size("sweep")
    came = lax.ppermute(renorm, "sweep", [(i, i + 1) for i in range(positions - 1)])
    psi = pl.pallas_call(
        psi_kernel,
        in_specs=[SMEM, VMEM],
        out_specs=HBM,
        out_shape=blocks,
        scratch_shapes=[PACKED, BLOCKS, dma(GROUPS, 1)],
        compiler_params=limit(8),
        cost_estimate=pl.CostEstimate(flops=10**7, bytes_accessed=4 * 10**6, transcendentals=0),
    )(meta, psi)
    came = lax.all_gather(came, "core", tiled=True)
    next_left = pl.pallas_call(
        shift_kernel,
        in_specs=[VMEM] * 2,
        out_specs=HBM,
        out_shape=blocks,
        scratch_shapes=[
            PACKED,
            BLOCKS,
            pltpu.VMEM((8, WIDTH), jnp.int32),
            pltpu.SMEM((8, WIDTH), jnp.int32),
            dma(GROUPS, 1),
            dma(1),
        ],
        compiler_params=limit(8),
    )(came, env)
    return psi[None], next_left[None]


def solution(mesh):
    positions = mesh.shape["sweep"]
    split = Mesh(
        mesh.devices.reshape(positions, ZH, ZL, X, 2), ("sweep", "zh", "zl", "x", "core")
    )
    ops = ("zh", "zl", "x", "core")
    return jax.shard_map(
        shards,
        mesh=split,
        in_specs=(
            P("sweep", None, None, None),
            P("sweep", ops, None, None, None),
            P("sweep", ops, None, None, None),
            P("sweep", ops, None),
            P("sweep", None),
            P("sweep", None, None, None),
        ),
        out_specs=(P("sweep", None, None, None), P("sweep", None, None, None)),
        check_vma=False,
    )
```

```python
import math

import jax
import jax.numpy as jnp
from jax import lax
from jax.experimental import pallas as pl
from jax.experimental.pallas import tpu as pltpu
from jax.sharding import Mesh, PartitionSpec as P

NSEC = 32
WIDTH = 128
PAIRS = 128
ROWS = 3 * NSEC * WIDTH // 4
HALF = ROWS // 2
TOTAL = NSEC * WIDTH * WIDTH
X, ZL, ZH = 4, 4, 4
NEAR = ZL * X
PIECE = HALF // NEAR
SCALE = 1.0 / math.sqrt(PAIRS)
GROUP = 8
GROUPS = NSEC // GROUP
FIRST_GROUP = 16
TAIL = 16
CHUNK = 256

VMEM = pl.BlockSpec(memory_space=pltpu.VMEM)
SMEM = pl.BlockSpec(memory_space=pltpu.SMEM)
HBM = pl.BlockSpec(memory_space=pltpu.HBM)
PACKED = pltpu.VMEM((ROWS + WIDTH, WIDTH), jnp.float32)
BLOCKS = pltpu.VMEM((NSEC, WIDTH, WIDTH), jnp.bfloat16)


def limit(mib):
    return pltpu.CompilerParams(vmem_limit_bytes=mib * 1024 * 1024)


def shape(dims, dtype):
    return jax.ShapeDtypeStruct(dims, dtype)


def square_mask(size):
    row = lax.broadcasted_iota(jnp.int32, (WIDTH, WIDTH), 0)
    col = lax.broadcasted_iota(jnp.int32, (WIDTH, WIDTH), 1)
    return (row < size) & (col < size)


def dot(a, b):
    return jnp.dot(a, b, preferred_element_type=jnp.float32)


def group_copies(pairs, sems, group=GROUP):
    return [
        [
            pltpu.make_async_copy(
                source.at[pl.ds(g * group, group)], target.at[pl.ds(g * group, group)], sems.at[g, k]
            )
            for k, (source, target) in enumerate(pairs)
        ]
        for g in range(NSEC // group)
    ]


def start_all(copies):
    for group in copies:
        for copy in group:
            copy.start()


def flat_sums(pairs):
    totals = None
    for start in range(0, ROWS, CHUNK):
        parts = [
            jnp.sum((p * q).reshape(CHUNK // 8, 8, WIDTH), axis=0)
            for p, q in pairs(pl.ds(start, CHUNK))
        ]
        totals = parts if totals is None else [t + p for t, p in zip(totals, parts)]
    return [jnp.sum(t, axis=(0, 1), keepdims=True) for t in totals]


def step_factors(x_of, sigma):
    def products(rows):
        x, s = x_of(rows), sigma[rows, :].astype(jnp.float32)
        return [(x, x), (x, s), (s, s)]

    xx, xs, ss = flat_sums(products)
    rho = xs / xx
    yy = xx + 0.64 * jnp.maximum(ss - rho * xs, 0.0)
    shrink = 1.0 / jnp.sqrt(yy / TOTAL + 1e-06)
    return (1.0 + 0.8 * rho) * shrink, 0.8 * shrink


def size_of(meta, i):
    return meta[2 + i]


def rows_below(size):
    return lax.broadcasted_iota(jnp.int32, (WIDTH, WIDTH), 0) < size


def run_pairs(meta, xb_of, left, right, env, group, ready, env_ready, packed, mine, other):
    sector = meta[1]
    column = lax.broadcasted_iota(jnp.int32, (WIDTH, WIDTH), 1)

    def body(g, carry):
        offset, at = carry
        ready(g)
        sums = []
        place = offset
        for j in range(group):
            i = g * group + j
            xb = xb_of(i, place)
            at = jnp.where(i == sector, place, at)
            place = place + size_of(meta, i)
            block = left[i]
            live = meta[2 + NSEC + i].astype(jnp.float32)
            u = live * dot(jnp.concatenate([block, block.T], 0), xb)
            u = u.astype(jnp.bfloat16)
            context = right[i]
            total = SCALE * dot(
                jnp.concatenate([u[:WIDTH], u[WIDTH:]], 1),
                jnp.concatenate([context.T, context], 0),
            )
            sums.append(jnp.where(column < size_of(meta, i), total, 0.0))
        for j in range(group):
            packed[pl.ds(offset, WIDTH), :] = sums[j]
            offset = offset + size_of(meta, g * group + j)
        return offset, at

    _, at = lax.fori_loop(0, NSEC // group, body, (jnp.int32(0), jnp.int32(0)))
    env_ready()
    term = 0.25 * dot(env[...], xb_of(sector, at, keep=False))
    packed[pl.ds(at, WIDTH), :] += jnp.where(square_mask(size_of(meta, sector)), term, 0.0)
    core = meta[0]
    mine[...] = packed[pl.ds(pl.multiple_of(core * HALF, 8), HALF), :]
    other[...] = packed[pl.ds(pl.multiple_of((1 - core) * HALF, 8), HALF), :].astype(jnp.bfloat16)


def first_kernel(
    meta, x0_in, left_in, right_in, env_in, mine, other, x_out,
    packed, x0, left, right, env, sems, env_sem, x_packed,
):
    pairs = [(x0_in, x0), (left_in, left), (right_in, right)]
    start_all(group_copies(pairs, sems, FIRST_GROUP))
    env_copy = pltpu.make_async_copy(env_in.at[meta[1]], env, env_sem.at[0])
    env_copy.start()

    def ready(g):
        some = pl.ds(g * FIRST_GROUP, FIRST_GROUP)
        for k, (source, target) in enumerate(pairs):
            pltpu.make_async_copy(source.at[some], target.at[some], sems.at[g, k]).wait()

    def xb_of(i, offset, keep=True):
        x = jnp.where(square_mask(size_of(meta, i)), x0[i].astype(jnp.float32), 0.0)
        if keep:
            x_packed[pl.ds(offset, WIDTH), :] = x
        return x.astype(jnp.bfloat16)

    run_pairs(meta, xb_of, left, right, env, FIRST_GROUP, ready, env_copy.wait, packed, mine, other)
    x_out[...] = x_packed[pl.ds(0, ROWS), :].astype(jnp.bfloat16)


def next_kernel(
    meta, sigma, x0, left, right, env_in, mine, other, factors, packed, env, env_sem, wide
):
    env_copy = pltpu.make_async_copy(env_in.at[meta[1]], env, env_sem.at[0])
    env_copy.start()

    def x_of(rows):
        return x0[rows, :].astype(jnp.float32)

    grow, drop = step_factors(x_of, sigma)
    factors[0:1, :] = jnp.broadcast_to(grow, (1, WIDTH))
    factors[1:2, :] = jnp.broadcast_to(drop, (1, WIDTH))
    wide[pl.ds(0, ROWS), :] = grow * x_of(pl.ds(0, ROWS)) - drop * sigma[...].astype(jnp.float32)

    def xb_of(i, offset, keep=True):
        mask = rows_below(size_of(meta, i))
        return jnp.where(mask, wide[pl.ds(offset, WIDTH), :], 0.0).astype(jnp.bfloat16)

    run_pairs(meta, xb_of, left, right, env, NSEC, lambda g: None, env_copy.wait, packed, mine, other)


def renorm_kernel(
    meta, factors, sigma_before, sigma, x0, env, psi_out, renorm_out, wide, packed
):
    grow_before, drop_before = factors[0:1, :], factors[1:2, :]

    def x_of(rows):
        return grow_before * x0[rows, :].astype(jnp.float32) - drop_before * sigma_before[
            rows, :
        ].astype(jnp.float32)

    grow, drop = step_factors(x_of, sigma)
    psi = grow * x_of(pl.ds(0, ROWS)) - drop * sigma[...].astype(jnp.float32)
    psi = psi.astype(jnp.bfloat16)
    psi_out[...] = psi
    wide[pl.ds(0, ROWS), :] = psi.astype(jnp.float32)
    low = pl.multiple_of(meta[0] * HALF, 8)
    offset = 0
    blocks = []
    for i in range(NSEC):
        block = jnp.where(rows_below(size_of(meta, i)), wide[pl.ds(offset, WIDTH), :], 0.0)
        block = block.astype(jnp.bfloat16)
        applied = dot(env[i], block).astype(jnp.bfloat16)
        blocks.append((offset, dot(block.T, applied) / math.sqrt(WIDTH)))
        offset = offset + size_of(meta, i)
    for place, block in blocks:
        packed[pl.ds(place, WIDTH), :] = block
    renorm_out[pl.ds(0, HALF), :] = packed[pl.ds(low, HALF), :].astype(jnp.bfloat16)
    lane = lax.broadcasted_iota(jnp.int32, (TAIL, WIDTH), 1)
    row = jnp.zeros((TAIL, WIDTH), jnp.int32)
    for i in range(NSEC):
        row = jnp.where(lane == i, size_of(meta, i), row)
    renorm_out[pl.ds(HALF, TAIL), :] = row.astype(jnp.float32).astype(jnp.bfloat16)


def unpack(size_at, wide, result, out, sems, finish):
    copies = group_copies([(result, out)], sems)
    offset = 0
    for g in range(GROUPS):
        for i in range(g * GROUP, (g + 1) * GROUP):
            size = size_at(i)
            block = jnp.where(rows_below(size), wide[pl.ds(offset, WIDTH), :], 0.0)
            result[i] = finish(i, block).astype(jnp.bfloat16)
            offset = offset + size
        copies[g][0].start()
    for group in copies:
        group[0].wait()


def psi_kernel(meta, psi, out, wide, result, sems):
    wide[pl.ds(0, ROWS), :] = psi[...].astype(jnp.float32)
    unpack(lambda i: size_of(meta, i), wide, result, out, sems, lambda i, block: block)


def shift_kernel(came, env, out, wide, result, numbers, sizes, sems, own_sem):
    numbers[...] = came[pl.ds(HALF, 8), :].astype(jnp.float32).astype(jnp.int32)
    sizes_copy = pltpu.make_async_copy(numbers, sizes, own_sem.at[0])
    sizes_copy.start()
    wide[pl.ds(0, HALF), :] = came[pl.ds(0, HALF), :].astype(jnp.float32)
    wide[pl.ds(HALF, HALF), :] = came[pl.ds(HALF + TAIL, HALF), :].astype(jnp.float32)
    sizes_copy.wait()
    unpack(
        lambda i: sizes[0, i],
        wide,
        result,
        out,
        sems,
        lambda i, block: env[i].astype(jnp.float32) + block,
    )


def sum_kernel(parts, out):
    total = jnp.sum(parts[...].astype(jnp.float32), axis=0).astype(jnp.bfloat16)
    for k in range(out.shape[0]):
        out[k] = total


def summed(parts, copies):
    return pl.pallas_call(
        sum_kernel,
        in_specs=[VMEM],
        out_specs=VMEM,
        out_shape=shape((copies,) + parts.shape[1:], parts.dtype),
        compiler_params=limit(4),
    )(parts)


def exchange(value, axes):
    return lax.all_to_all(value, axes, 0, 0)


def all_summed(mine, other):
    both = lax.all_gather(other, "core")
    came = lax.dynamic_index_in_dim(both, 1 - lax.axis_index("core"), keepdims=False)
    chip = (mine + came.astype(jnp.float32)).astype(jnp.bfloat16).reshape(NEAR, PIECE, WIDTH)
    near = summed(exchange(chip, ("zl", "x")), ZH)
    far = summed(exchange(near, "zh"), NEAR)
    half = exchange(far, ("zl", "x"))
    return lax.all_gather(half.reshape(HALF, WIDTH), "core", tiled=True)


def dma(*dims):
    return pltpu.SemaphoreType.DMA(dims)


def shards(initial_trial_state, left_ops, right_ops, pair_sectors, sector_size, left_env):
    x0 = initial_trial_state[0]
    left = left_ops[0, 0]
    right = right_ops[0, 0]
    env = left_env[0]
    core = lax.axis_index("core")
    sector = lax.axis_index(("zh", "zl", "x", "core")) // (PAIRS // NSEC)
    own = jnp.stack([core, sector]).astype(jnp.int32)
    meta = jnp.concatenate([own, sector_size[0], pair_sectors[0, 0]])

    sums = [shape((HALF, WIDTH), jnp.float32), shape((HALF, WIDTH), jnp.bfloat16)]
    rows = shape((ROWS, WIDTH), jnp.bfloat16)
    blocks = shape((NSEC, WIDTH, WIDTH), jnp.bfloat16)
    env_scratch = [pltpu.VMEM((WIDTH, WIDTH), jnp.bfloat16)]
    mine, other, x0 = pl.pallas_call(
        first_kernel,
        in_specs=[SMEM] + [HBM] * 4,
        out_specs=[VMEM] * 3,
        out_shape=sums + [rows],
        scratch_shapes=[PACKED, BLOCKS, BLOCKS, BLOCKS]
        + env_scratch
        + [dma(NSEC // FIRST_GROUP, 3), dma(1), PACKED],
        compiler_params=limit(52),
    )(meta, x0, left, right, env)
    before = all_summed(mine, other)
    mine, other, factors = pl.pallas_call(
        next_kernel,
        in_specs=[SMEM] + [VMEM] * 4 + [HBM],
        out_specs=[VMEM] * 3,
        out_shape=sums + [shape((2, WIDTH), jnp.float32)],
        scratch_shapes=[PACKED] + env_scratch + [dma(1), PACKED],
        compiler_params=limit(12),
    )(meta, before, x0, left, right, env)
    sigma = all_summed(mine, other)
    psi, renorm = pl.pallas_call(
        renorm_kernel,
        in_specs=[SMEM] + [VMEM] * 5,
        out_specs=[VMEM] * 2,
        out_shape=[rows, shape((HALF + TAIL, WIDTH), jnp.bfloat16)],
        scratch_shapes=[PACKED, PACKED],
        compiler_params=limit(12),
    )(meta, factors, before, sigma, x0, env)
    positions = lax.axis_size("sweep")
    came = lax.ppermute(renorm, "sweep", [(i, i + 1) for i in range(positions - 1)])
    psi = pl.pallas_call(
        psi_kernel,
        in_specs=[SMEM, VMEM],
        out_specs=HBM,
        out_shape=blocks,
        scratch_shapes=[PACKED, BLOCKS, dma(GROUPS, 1)],
        compiler_params=limit(8),
        cost_estimate=pl.CostEstimate(flops=10**7, bytes_accessed=4 * 10**6, transcendentals=0),
    )(meta, psi)
    came = lax.all_gather(came, "core", tiled=True)
    next_left = pl.pallas_call(
        shift_kernel,
        in_specs=[VMEM] * 2,
        out_specs=HBM,
        out_shape=blocks,
        scratch_shapes=[
            PACKED,
            BLOCKS,
            pltpu.VMEM((8, WIDTH), jnp.int32),
            pltpu.SMEM((8, WIDTH), jnp.int32),
            dma(GROUPS, 1),
            dma(1),
        ],
        compiler_params=limit(8),
    )(came, env)
    return psi[None], next_left[None]


def solution(mesh):
    positions = mesh.shape["sweep"]
    split = Mesh(
        mesh.devices.reshape(positions, ZH, ZL, X, 2), ("sweep", "zh", "zl", "x", "core")
    )
    ops = ("zh", "zl", "x", "core")
    return jax.shard_map(
        shards,
        mesh=split,
        in_specs=(
            P("sweep", None, None, None),
            P("sweep", ops, None, None, None),
            P("sweep", ops, None, None, None),
            P("sweep", ops, None),
            P("sweep", None),
            P("sweep", None, None, None),
        ),
        out_specs=(P("sweep", None, None, None), P("sweep", None, None, None)),
        check_vma=False,
    )
```

```python
import math

import jax
import jax.numpy as jnp
from jax import lax
from jax.experimental import pallas as pl
from jax.experimental.pallas import tpu as pltpu
from jax.sharding import Mesh, PartitionSpec as P

NSEC = 32
WIDTH = 128
PAIRS = 128
ROWS = 3 * NSEC * WIDTH // 4
HALF = ROWS // 2
TOTAL = NSEC * WIDTH * WIDTH
X, ZL, ZH = 4, 4, 4
NEAR = ZL * X
PIECE = HALF // NEAR
SCALE = 1.0 / math.sqrt(PAIRS)
GROUP = 8
GROUPS = NSEC // GROUP
FIRST_GROUP = 16
REACH = NSEC - HALF // WIDTH
TAIL = 16
CHUNK = 256

VMEM = pl.BlockSpec(memory_space=pltpu.VMEM)
SMEM = pl.BlockSpec(memory_space=pltpu.SMEM)
HBM = pl.BlockSpec(memory_space=pltpu.HBM)
PACKED = pltpu.VMEM((ROWS + WIDTH, WIDTH), jnp.float32)
BLOCKS = pltpu.VMEM((NSEC, WIDTH, WIDTH), jnp.bfloat16)


def limit(mib):
    return pltpu.CompilerParams(vmem_limit_bytes=mib * 1024 * 1024)


def shape(dims, dtype):
    return jax.ShapeDtypeStruct(dims, dtype)


def square_mask(size):
    row = lax.broadcasted_iota(jnp.int32, (WIDTH, WIDTH), 0)
    col = lax.broadcasted_iota(jnp.int32, (WIDTH, WIDTH), 1)
    return (row < size) & (col < size)


def dot(a, b):
    return jnp.dot(a, b, preferred_element_type=jnp.float32)


def group_copies(pairs, sems, group=GROUP):
    return [
        [
            pltpu.make_async_copy(
                source.at[pl.ds(g * group, group)], target.at[pl.ds(g * group, group)], sems.at[g, k]
            )
            for k, (source, target) in enumerate(pairs)
        ]
        for g in range(NSEC // group)
    ]


def start_all(copies):
    for group in copies:
        for copy in group:
            copy.start()


def flat_sums(pairs):
    totals = None
    for start in range(0, ROWS, CHUNK):
        parts = [
            jnp.sum((p * q).reshape(CHUNK // 8, 8, WIDTH), axis=0)
            for p, q in pairs(pl.ds(start, CHUNK))
        ]
        totals = parts if totals is None else [t + p for t, p in zip(totals, parts)]
    return [jnp.sum(t, axis=(0, 1), keepdims=True) for t in totals]


def step_factors(x_of, sigma):
    def products(rows):
        x, s = x_of(rows), sigma[rows, :].astype(jnp.float32)
        return [(x, x), (x, s), (s, s)]

    xx, xs, ss = flat_sums(products)
    rho = xs / xx
    yy = xx + 0.64 * jnp.maximum(ss - rho * xs, 0.0)
    shrink = 1.0 / jnp.sqrt(yy / TOTAL + 1e-06)
    return (1.0 + 0.8 * rho) * shrink, 0.8 * shrink


def size_of(meta, i):
    return meta[2 + i]


def rows_below(size):
    return lax.broadcasted_iota(jnp.int32, (WIDTH, WIDTH), 0) < size


def run_pairs(meta, xb_of, left, right, env, group, ready, env_ready, packed, mine, other):
    sector = meta[1]
    column = lax.broadcasted_iota(jnp.int32, (WIDTH, WIDTH), 1)

    def body(g, carry):
        offset, at = carry
        ready(g)
        sums = []
        place = offset
        for j in range(group):
            i = g * group + j
            xb = xb_of(i, place)
            at = jnp.where(i == sector, place, at)
            place = place + size_of(meta, i)
            block = left[i]
            live = meta[2 + NSEC + i].astype(jnp.float32)
            u = live * dot(jnp.concatenate([block, block.T], 0), xb)
            u = u.astype(jnp.bfloat16)
            context = right[i]
            total = SCALE * dot(
                jnp.concatenate([u[:WIDTH], u[WIDTH:]], 1),
                jnp.concatenate([context.T, context], 0),
            )
            sums.append(jnp.where(column < size_of(meta, i), total, 0.0))
        for j in range(group):
            packed[pl.ds(offset, WIDTH), :] = sums[j]
            offset = offset + size_of(meta, g * group + j)
        return offset, at

    _, at = lax.fori_loop(0, NSEC // group, body, (jnp.int32(0), jnp.int32(0)))
    env_ready()
    term = 0.25 * dot(env[...], xb_of(sector, at, keep=False))
    packed[pl.ds(at, WIDTH), :] += jnp.where(square_mask(size_of(meta, sector)), term, 0.0)
    core = meta[0]
    mine[...] = packed[pl.ds(pl.multiple_of(core * HALF, 8), HALF), :]
    other[...] = packed[pl.ds(pl.multiple_of((1 - core) * HALF, 8), HALF), :].astype(jnp.bfloat16)


def first_kernel(
    meta, x0_in, left_in, right_in, env_in, mine, other, x_out,
    packed, x0, left, right, env, sems, env_sem, x_packed,
):
    pairs = [(x0_in, x0), (left_in, left), (right_in, right)]
    start_all(group_copies(pairs, sems, FIRST_GROUP))
    env_copy = pltpu.make_async_copy(env_in.at[meta[1]], env, env_sem.at[0])
    env_copy.start()

    def ready(g):
        some = pl.ds(g * FIRST_GROUP, FIRST_GROUP)
        for k, (source, target) in enumerate(pairs):
            pltpu.make_async_copy(source.at[some], target.at[some], sems.at[g, k]).wait()

    def xb_of(i, offset, keep=True):
        x = jnp.where(square_mask(size_of(meta, i)), x0[i].astype(jnp.float32), 0.0)
        if keep:
            x_packed[pl.ds(offset, WIDTH), :] = x
        return x.astype(jnp.bfloat16)

    run_pairs(meta, xb_of, left, right, env, FIRST_GROUP, ready, env_copy.wait, packed, mine, other)
    x_out[...] = x_packed[pl.ds(0, ROWS), :].astype(jnp.bfloat16)


def next_kernel(
    meta, sigma, x0, left, right, env_in, mine, other, factors, packed, env, env_sem, wide
):
    env_copy = pltpu.make_async_copy(env_in.at[meta[1]], env, env_sem.at[0])
    env_copy.start()

    def x_of(rows):
        return x0[rows, :].astype(jnp.float32)

    grow, drop = step_factors(x_of, sigma)
    factors[0:1, :] = jnp.broadcast_to(grow, (1, WIDTH))
    factors[1:2, :] = jnp.broadcast_to(drop, (1, WIDTH))
    wide[pl.ds(0, ROWS), :] = grow * x_of(pl.ds(0, ROWS)) - drop * sigma[...].astype(jnp.float32)

    def xb_of(i, offset, keep=True):
        mask = rows_below(size_of(meta, i))
        return jnp.where(mask, wide[pl.ds(offset, WIDTH), :], 0.0).astype(jnp.bfloat16)

    run_pairs(meta, xb_of, left, right, env, NSEC, lambda g: None, env_copy.wait, packed, mine, other)


def second_state(factors, x0, sigma_before):
    grow, drop = factors[0:1, :], factors[1:2, :]

    def x_of(rows):
        return grow * x0[rows, :].astype(jnp.float32) - drop * sigma_before[rows, :].astype(
            jnp.float32
        )

    return x_of


def renorm_kernel(
    meta, factors, sigma_before, sigma, x0, env, factors_out, renorm_out, wide, packed
):
    x_of = second_state(factors, x0, sigma_before)
    grow, drop = step_factors(x_of, sigma)
    factors_out[0:1, :] = jnp.broadcast_to(grow, (1, WIDTH))
    factors_out[1:2, :] = jnp.broadcast_to(drop, (1, WIDTH))
    core = meta[0]
    near = pl.ds(pl.multiple_of(core * (HALF - WIDTH), 16), HALF + WIDTH)
    psi = grow * x_of(near) - drop * sigma[near, :].astype(jnp.float32)
    wide[near, :] = psi.astype(jnp.bfloat16).astype(jnp.float32)
    first = core * (NSEC - REACH)
    offset = lax.fori_loop(0, first, lambda i, total: total + size_of(meta, i), jnp.int32(0))
    blocks = []
    for j in range(REACH):
        i = first + j
        block = jnp.where(rows_below(size_of(meta, i)), wide[pl.ds(offset, WIDTH), :], 0.0)
        block = block.astype(jnp.bfloat16)
        applied = dot(env[i], block).astype(jnp.bfloat16)
        blocks.append((offset, dot(block.T, applied) / math.sqrt(WIDTH)))
        offset = offset + size_of(meta, i)
    for place, block in blocks:
        packed[pl.ds(place, WIDTH), :] = block
    renorm_out[pl.ds(0, HALF), :] = packed[
        pl.ds(pl.multiple_of(core * HALF, 8), HALF), :
    ].astype(jnp.bfloat16)
    lane = lax.broadcasted_iota(jnp.int32, (TAIL, WIDTH), 1)
    row = jnp.zeros((TAIL, WIDTH), jnp.int32)
    for i in range(NSEC):
        row = jnp.where(lane == i, size_of(meta, i), row)
    renorm_out[pl.ds(HALF, TAIL), :] = row.astype(jnp.float32).astype(jnp.bfloat16)


def unpack(size_at, wide, result, out, sems, finish):
    copies = group_copies([(result, out)], sems)
    offset = 0
    for g in range(GROUPS):
        for i in range(g * GROUP, (g + 1) * GROUP):
            size = size_at(i)
            block = jnp.where(rows_below(size), wide[pl.ds(offset, WIDTH), :], 0.0)
            result[i] = finish(i, block).astype(jnp.bfloat16)
            offset = offset + size
        copies[g][0].start()
    for group in copies:
        group[0].wait()


def psi_kernel(meta, factors, factors_last, sigma_before, sigma, x0, out, wide, result, sems):
    grow, drop = factors_last[0:1, :], factors_last[1:2, :]
    rows = pl.ds(0, ROWS)
    x = second_state(factors, x0, sigma_before)(rows)
    wide[rows, :] = grow * x - drop * sigma[...].astype(jnp.float32)
    unpack(lambda i: size_of(meta, i), wide, result, out, sems, lambda i, block: block)


def shift_kernel(came, env, out, wide, result, numbers, sizes, sems, own_sem):
    numbers[...] = came[pl.ds(HALF, 8), :].astype(jnp.float32).astype(jnp.int32)
    sizes_copy = pltpu.make_async_copy(numbers, sizes, own_sem.at[0])
    sizes_copy.start()
    wide[pl.ds(0, HALF), :] = came[pl.ds(0, HALF), :].astype(jnp.float32)
    wide[pl.ds(HALF, HALF), :] = came[pl.ds(HALF + TAIL, HALF), :].astype(jnp.float32)
    sizes_copy.wait()
    unpack(
        lambda i: sizes[0, i],
        wide,
        result,
        out,
        sems,
        lambda i, block: env[i].astype(jnp.float32) + block,
    )


def sum_kernel(parts, out):
    total = jnp.sum(parts[...].astype(jnp.float32), axis=0).astype(jnp.bfloat16)
    for k in range(out.shape[0]):
        out[k] = total


def summed(parts, copies):
    return pl.pallas_call(
        sum_kernel,
        in_specs=[VMEM],
        out_specs=VMEM,
        out_shape=shape((copies,) + parts.shape[1:], parts.dtype),
        compiler_params=limit(4),
    )(parts)


def exchange(value, axes):
    return lax.all_to_all(value, axes, 0, 0)


def all_summed(mine, other):
    both = lax.all_gather(other, "core")
    came = lax.dynamic_index_in_dim(both, 1 - lax.axis_index("core"), keepdims=False)
    chip = (mine + came.astype(jnp.float32)).astype(jnp.bfloat16).reshape(NEAR, PIECE, WIDTH)
    near = summed(exchange(chip, ("zl", "x")), ZH)
    far = summed(exchange(near, "zh"), NEAR)
    half = exchange(far, ("zl", "x"))
    return lax.all_gather(half.reshape(HALF, WIDTH), "core", tiled=True)


def dma(*dims):
    return pltpu.SemaphoreType.DMA(dims)


def shards(initial_trial_state, left_ops, right_ops, pair_sectors, sector_size, left_env):
    x0 = initial_trial_state[0]
    left = left_ops[0, 0]
    right = right_ops[0, 0]
    env = left_env[0]
    core = lax.axis_index("core")
    sector = lax.axis_index(("zh", "zl", "x", "core")) // (PAIRS // NSEC)
    own = jnp.stack([core, sector]).astype(jnp.int32)
    meta = jnp.concatenate([own, sector_size[0], pair_sectors[0, 0]])

    sums = [shape((HALF, WIDTH), jnp.float32), shape((HALF, WIDTH), jnp.bfloat16)]
    rows = shape((ROWS, WIDTH), jnp.bfloat16)
    blocks = shape((NSEC, WIDTH, WIDTH), jnp.bfloat16)
    env_scratch = [pltpu.VMEM((WIDTH, WIDTH), jnp.bfloat16)]
    mine, other, x0 = pl.pallas_call(
        first_kernel,
        in_specs=[SMEM] + [HBM] * 4,
        out_specs=[VMEM] * 3,
        out_shape=sums + [rows],
        scratch_shapes=[PACKED, BLOCKS, BLOCKS, BLOCKS]
        + env_scratch
        + [dma(NSEC // FIRST_GROUP, 3), dma(1), PACKED],
        compiler_params=limit(52),
    )(meta, x0, left, right, env)
    before = all_summed(mine, other)
    mine, other, factors = pl.pallas_call(
        next_kernel,
        in_specs=[SMEM] + [VMEM] * 4 + [HBM],
        out_specs=[VMEM] * 3,
        out_shape=sums + [shape((2, WIDTH), jnp.float32)],
        scratch_shapes=[PACKED] + env_scratch + [dma(1), PACKED],
        compiler_params=limit(12),
    )(meta, before, x0, left, right, env)
    sigma = all_summed(mine, other)
    factors_last, renorm = pl.pallas_call(
        renorm_kernel,
        in_specs=[SMEM] + [VMEM] * 5,
        out_specs=[VMEM] * 2,
        out_shape=[
            shape((2, WIDTH), jnp.float32),
            shape((HALF + TAIL, WIDTH), jnp.bfloat16),
        ],
        scratch_shapes=[PACKED, PACKED],
        compiler_params=limit(12),
    )(meta, factors, before, sigma, x0, env)
    positions = lax.axis_size("sweep")
    came = lax.ppermute(renorm, "sweep", [(i, i + 1) for i in range(positions - 1)])
    psi = pl.pallas_call(
        psi_kernel,
        in_specs=[SMEM] + [VMEM] * 5,
        out_specs=HBM,
        out_shape=blocks,
        scratch_shapes=[PACKED, BLOCKS, dma(GROUPS, 1)],
        compiler_params=limit(8),
        cost_estimate=pl.CostEstimate(flops=10**7, bytes_accessed=4 * 10**6, transcendentals=0),
    )(meta, factors, factors_last, before, sigma, x0)
    came = lax.all_gather(came, "core", tiled=True)
    next_left = pl.pallas_call(
        shift_kernel,
        in_specs=[VMEM] * 2,
        out_specs=HBM,
        out_shape=blocks,
        scratch_shapes=[
            PACKED,
            BLOCKS,
            pltpu.VMEM((8, WIDTH), jnp.int32),
            pltpu.SMEM((8, WIDTH), jnp.int32),
            dma(GROUPS, 1),
            dma(1),
        ],
        compiler_params=limit(8),
    )(came, env)
    return psi[None], next_left[None]


def solution(mesh):
    positions = mesh.shape["sweep"]
    split = Mesh(
        mesh.devices.reshape(positions, ZH, ZL, X, 2), ("sweep", "zh", "zl", "x", "core")
    )
    ops = ("zh", "zl", "x", "core")
    return jax.shard_map(
        shards,
        mesh=split,
        in_specs=(
            P("sweep", None, None, None),
            P("sweep", ops, None, None, None),
            P("sweep", ops, None, None, None),
            P("sweep", ops, None),
            P("sweep", None),
            P("sweep", None, None, None),
        ),
        out_specs=(P("sweep", None, None, None), P("sweep", None, None, None)),
        check_vma=False,
    )
```

```python
import math

import jax
import jax.numpy as jnp
from jax import lax
from jax.experimental import pallas as pl
from jax.experimental.pallas import tpu as pltpu
from jax.sharding import Mesh, PartitionSpec as P

NSEC = 32
WIDTH = 128
PAIRS = 128
ROWS = 3 * NSEC * WIDTH // 4
HALF = ROWS // 2
TOTAL = NSEC * WIDTH * WIDTH
X, ZL, ZH = 4, 4, 4
NEAR = ZL * X
PIECE = HALF // NEAR
SCALE = 1.0 / math.sqrt(PAIRS)
GROUP = 8
GROUPS = NSEC // GROUP
FIRST_GROUP = 16
REACH = NSEC - HALF // WIDTH
TAIL = 16
CHUNK = 256

VMEM = pl.BlockSpec(memory_space=pltpu.VMEM)
SMEM = pl.BlockSpec(memory_space=pltpu.SMEM)
HBM = pl.BlockSpec(memory_space=pltpu.HBM)
PACKED = pltpu.VMEM((ROWS + WIDTH, WIDTH), jnp.float32)
BLOCKS = pltpu.VMEM((NSEC, WIDTH, WIDTH), jnp.bfloat16)


def limit(mib):
    return pltpu.CompilerParams(vmem_limit_bytes=mib * 1024 * 1024)


def shape(dims, dtype):
    return jax.ShapeDtypeStruct(dims, dtype)


def square_mask(size):
    row = lax.broadcasted_iota(jnp.int32, (WIDTH, WIDTH), 0)
    col = lax.broadcasted_iota(jnp.int32, (WIDTH, WIDTH), 1)
    return (row < size) & (col < size)


def dot(a, b):
    return jnp.dot(a, b, preferred_element_type=jnp.float32)


def group_copies(pairs, sems, group=GROUP):
    return [
        [
            pltpu.make_async_copy(
                source.at[pl.ds(g * group, group)], target.at[pl.ds(g * group, group)], sems.at[g, k]
            )
            for k, (source, target) in enumerate(pairs)
        ]
        for g in range(NSEC // group)
    ]


def start_all(copies):
    for group in copies:
        for copy in group:
            copy.start()


def flat_sums(pairs):
    totals = None
    for start in range(0, ROWS, CHUNK):
        parts = [
            jnp.sum((p * q).reshape(CHUNK // 8, 8, WIDTH), axis=0)
            for p, q in pairs(pl.ds(start, CHUNK))
        ]
        totals = parts if totals is None else [t + p for t, p in zip(totals, parts)]
    return [jnp.sum(t, axis=(0, 1), keepdims=True) for t in totals]


def step_factors(x, sigma):
    def products(rows):
        xs, s = x[rows, :].astype(jnp.float32), sigma[rows, :].astype(jnp.float32)
        return [(xs, xs), (xs, s), (s, s)]

    xx, xs, ss = flat_sums(products)
    rho = xs / xx
    yy = xx + 0.64 * jnp.maximum(ss - rho * xs, 0.0)
    shrink = 1.0 / jnp.sqrt(yy / TOTAL + 1e-06)
    return (1.0 + 0.8 * rho) * shrink, 0.8 * shrink


def size_of(meta, i):
    return meta[2 + i]


def rows_below(size):
    return lax.broadcasted_iota(jnp.int32, (WIDTH, WIDTH), 0) < size


def run_pairs(meta, xb_of, left, right, env, group, ready, env_ready, packed, mine, other):
    sector = meta[1]
    column = lax.broadcasted_iota(jnp.int32, (WIDTH, WIDTH), 1)

    def body(g, carry):
        offset, at = carry
        ready(g)
        sums = []
        place = offset
        for j in range(group):
            i = g * group + j
            xb = xb_of(i, place)
            at = jnp.where(i == sector, place, at)
            place = place + size_of(meta, i)
            block = left[i]
            live = meta[2 + NSEC + i].astype(jnp.float32)
            u = live * dot(jnp.concatenate([block, block.T], 0), xb)
            u = u.astype(jnp.bfloat16)
            context = right[i]
            total = SCALE * dot(
                jnp.concatenate([u[:WIDTH], u[WIDTH:]], 1),
                jnp.concatenate([context.T, context], 0),
            )
            sums.append(jnp.where(column < size_of(meta, i), total, 0.0))
        for j in range(group):
            packed[pl.ds(offset, WIDTH), :] = sums[j]
            offset = offset + size_of(meta, g * group + j)
        return offset, at

    _, at = lax.fori_loop(0, NSEC // group, body, (jnp.int32(0), jnp.int32(0)))
    env_ready()
    term = 0.25 * dot(env[...], xb_of(sector, at, keep=False))
    packed[pl.ds(at, WIDTH), :] += jnp.where(square_mask(size_of(meta, sector)), term, 0.0)
    core = meta[0]
    mine[...] = packed[pl.ds(pl.multiple_of(core * HALF, 8), HALF), :]
    other[...] = packed[pl.ds(pl.multiple_of((1 - core) * HALF, 8), HALF), :].astype(jnp.bfloat16)


def first_kernel(
    meta, x0_in, left_in, right_in, env_in, mine, other, x_out,
    packed, x0, left, right, env, sems, env_sem, x_packed,
):
    pairs = [(x0_in, x0), (left_in, left), (right_in, right)]
    start_all(group_copies(pairs, sems, FIRST_GROUP))
    env_copy = pltpu.make_async_copy(env_in.at[meta[1]], env, env_sem.at[0])
    env_copy.start()

    def ready(g):
        some = pl.ds(g * FIRST_GROUP, FIRST_GROUP)
        for k, (source, target) in enumerate(pairs):
            pltpu.make_async_copy(source.at[some], target.at[some], sems.at[g, k]).wait()

    def xb_of(i, offset, keep=True):
        x = jnp.where(square_mask(size_of(meta, i)), x0[i].astype(jnp.float32), 0.0)
        if keep:
            x_packed[pl.ds(offset, WIDTH), :] = x
        return x.astype(jnp.bfloat16)

    run_pairs(meta, xb_of, left, right, env, FIRST_GROUP, ready, env_copy.wait, packed, mine, other)
    x_out[...] = x_packed[pl.ds(0, ROWS), :].astype(jnp.bfloat16)


def next_kernel(
    meta, sigma, x0, left, right, env_in, mine, other, wide, packed, env, env_sem
):
    env_copy = pltpu.make_async_copy(env_in.at[meta[1]], env, env_sem.at[0])
    env_copy.start()

    rows = pl.ds(0, ROWS)
    grow, drop = step_factors(x0, sigma)
    wide[rows, :] = grow * x0[...].astype(jnp.float32) - drop * sigma[...].astype(jnp.float32)

    def xb_of(i, offset, keep=True):
        mask = rows_below(size_of(meta, i))
        return jnp.where(mask, wide[pl.ds(offset, WIDTH), :], 0.0).astype(jnp.bfloat16)

    run_pairs(meta, xb_of, left, right, env, NSEC, lambda g: None, env_copy.wait, packed, mine, other)


def renorm_kernel(
    meta, x, sigma, env, factors_out, renorm_out, wide, packed
):
    grow, drop = step_factors(x, sigma)
    factors_out[0:1, :] = jnp.broadcast_to(grow, (1, WIDTH))
    factors_out[1:2, :] = jnp.broadcast_to(drop, (1, WIDTH))
    core = meta[0]
    near = pl.ds(pl.multiple_of(core * (HALF - WIDTH), 16), HALF + WIDTH)
    psi = grow * x[near, :] - drop * sigma[near, :].astype(jnp.float32)
    wide[near, :] = psi.astype(jnp.bfloat16).astype(jnp.float32)
    first = core * (NSEC - REACH)
    offset = lax.fori_loop(0, first, lambda i, total: total + size_of(meta, i), jnp.int32(0))
    blocks = []
    for j in range(REACH):
        i = first + j
        block = jnp.where(rows_below(size_of(meta, i)), wide[pl.ds(offset, WIDTH), :], 0.0)
        block = block.astype(jnp.bfloat16)
        applied = dot(env[i], block).astype(jnp.bfloat16)
        blocks.append((offset, dot(block.T, applied) / math.sqrt(WIDTH)))
        offset = offset + size_of(meta, i)
    for place, block in blocks:
        packed[pl.ds(place, WIDTH), :] = block
    renorm_out[pl.ds(0, HALF), :] = packed[
        pl.ds(pl.multiple_of(core * HALF, 8), HALF), :
    ].astype(jnp.bfloat16)
    lane = lax.broadcasted_iota(jnp.int32, (TAIL, WIDTH), 1)
    row = jnp.zeros((TAIL, WIDTH), jnp.int32)
    for i in range(NSEC):
        row = jnp.where(lane == i, size_of(meta, i), row)
    renorm_out[pl.ds(HALF, TAIL), :] = row.astype(jnp.float32).astype(jnp.bfloat16)


def unpack(size_at, wide, result, out, sems, finish):
    copies = group_copies([(result, out)], sems)
    offset = 0
    for g in range(GROUPS):
        for i in range(g * GROUP, (g + 1) * GROUP):
            size = size_at(i)
            block = jnp.where(rows_below(size), wide[pl.ds(offset, WIDTH), :], 0.0)
            result[i] = finish(i, block).astype(jnp.bfloat16)
            offset = offset + size
        copies[g][0].start()
    for group in copies:
        group[0].wait()


def psi_kernel(meta, factors, x, sigma, out, wide, result, sems):
    grow, drop = factors[0:1, :], factors[1:2, :]
    rows = pl.ds(0, ROWS)
    wide[rows, :] = grow * x[rows, :] - drop * sigma[...].astype(jnp.float32)
    unpack(lambda i: size_of(meta, i), wide, result, out, sems, lambda i, block: block)


def shift_kernel(came, env, out, wide, result, numbers, sizes, sems, own_sem):
    numbers[...] = came[pl.ds(HALF, 8), :].astype(jnp.float32).astype(jnp.int32)
    sizes_copy = pltpu.make_async_copy(numbers, sizes, own_sem.at[0])
    sizes_copy.start()
    wide[pl.ds(0, HALF), :] = came[pl.ds(0, HALF), :].astype(jnp.float32)
    wide[pl.ds(HALF, HALF), :] = came[pl.ds(HALF + TAIL, HALF), :].astype(jnp.float32)
    sizes_copy.wait()
    unpack(
        lambda i: sizes[0, i],
        wide,
        result,
        out,
        sems,
        lambda i, block: env[i].astype(jnp.float32) + block,
    )


def sum_kernel(parts, out):
    total = jnp.sum(parts[...].astype(jnp.float32), axis=0).astype(jnp.bfloat16)
    for k in range(out.shape[0]):
        out[k] = total


def summed(parts, copies):
    return pl.pallas_call(
        sum_kernel,
        in_specs=[VMEM],
        out_specs=VMEM,
        out_shape=shape((copies,) + parts.shape[1:], parts.dtype),
        compiler_params=limit(4),
    )(parts)


def exchange(value, axes):
    return lax.all_to_all(value, axes, 0, 0)


def all_summed(mine, other):
    both = lax.all_gather(other, "core")
    came = lax.dynamic_index_in_dim(both, 1 - lax.axis_index("core"), keepdims=False)
    chip = (mine + came.astype(jnp.float32)).astype(jnp.bfloat16).reshape(NEAR, PIECE, WIDTH)
    near = summed(exchange(chip, ("zl", "x")), ZH)
    far = summed(exchange(near, "zh"), NEAR)
    half = exchange(far, ("zl", "x"))
    return lax.all_gather(half.reshape(HALF, WIDTH), "core", tiled=True)


def dma(*dims):
    return pltpu.SemaphoreType.DMA(dims)


def shards(initial_trial_state, left_ops, right_ops, pair_sectors, sector_size, left_env):
    x0 = initial_trial_state[0]
    left = left_ops[0, 0]
    right = right_ops[0, 0]
    env = left_env[0]
    core = lax.axis_index("core")
    sector = lax.axis_index(("zh", "zl", "x", "core")) // (PAIRS // NSEC)
    own = jnp.stack([core, sector]).astype(jnp.int32)
    meta = jnp.concatenate([own, sector_size[0], pair_sectors[0, 0]])

    sums = [shape((HALF, WIDTH), jnp.float32), shape((HALF, WIDTH), jnp.bfloat16)]
    state = shape((ROWS + WIDTH, WIDTH), jnp.float32)
    blocks = shape((NSEC, WIDTH, WIDTH), jnp.bfloat16)
    env_scratch = [pltpu.VMEM((WIDTH, WIDTH), jnp.bfloat16)]
    mine, other, x0 = pl.pallas_call(
        first_kernel,
        in_specs=[SMEM] + [HBM] * 4,
        out_specs=[VMEM] * 3,
        out_shape=sums + [shape((ROWS, WIDTH), jnp.bfloat16)],
        scratch_shapes=[PACKED, BLOCKS, BLOCKS, BLOCKS]
        + env_scratch
        + [dma(NSEC // FIRST_GROUP, 3), dma(1), PACKED],
        compiler_params=limit(52),
    )(meta, x0, left, right, env)
    sigma = all_summed(mine, other)
    mine, other, x = pl.pallas_call(
        next_kernel,
        in_specs=[SMEM] + [VMEM] * 4 + [HBM],
        out_specs=[VMEM] * 3,
        out_shape=sums + [state],
        scratch_shapes=[PACKED] + env_scratch + [dma(1)],
        compiler_params=limit(12),
    )(meta, sigma, x0, left, right, env)
    sigma = all_summed(mine, other)
    factors, renorm = pl.pallas_call(
        renorm_kernel,
        in_specs=[SMEM] + [VMEM] * 3,
        out_specs=[VMEM] * 2,
        out_shape=[
            shape((2, WIDTH), jnp.float32),
            shape((HALF + TAIL, WIDTH), jnp.bfloat16),
        ],
        scratch_shapes=[PACKED, PACKED],
        compiler_params=limit(12),
    )(meta, x, sigma, env)
    positions = lax.axis_size("sweep")
    came = lax.ppermute(renorm, "sweep", [(i, i + 1) for i in range(positions - 1)])
    psi = pl.pallas_call(
        psi_kernel,
        in_specs=[SMEM] + [VMEM] * 3,
        out_specs=HBM,
        out_shape=blocks,
        scratch_shapes=[PACKED, BLOCKS, dma(GROUPS, 1)],
        compiler_params=limit(8),
        cost_estimate=pl.CostEstimate(flops=10**7, bytes_accessed=4 * 10**6, transcendentals=0),
    )(meta, factors, x, sigma)
    came = lax.all_gather(came, "core", tiled=True)
    next_left = pl.pallas_call(
        shift_kernel,
        in_specs=[VMEM] * 2,
        out_specs=HBM,
        out_shape=blocks,
        scratch_shapes=[
            PACKED,
            BLOCKS,
            pltpu.VMEM((8, WIDTH), jnp.int32),
            pltpu.SMEM((8, WIDTH), jnp.int32),
            dma(GROUPS, 1),
            dma(1),
        ],
        compiler_params=limit(8),
    )(came, env)
    return psi[None], next_left[None]


def solution(mesh):
    positions = mesh.shape["sweep"]
    split = Mesh(
        mesh.devices.reshape(positions, ZH, ZL, X, 2), ("sweep", "zh", "zl", "x", "core")
    )
    ops = ("zh", "zl", "x", "core")
    return jax.shard_map(
        shards,
        mesh=split,
        in_specs=(
            P("sweep", None, None, None),
            P("sweep", ops, None, None, None),
            P("sweep", ops, None, None, None),
            P("sweep", ops, None),
            P("sweep", None),
            P("sweep", None, None, None),
        ),
        out_specs=(P("sweep", None, None, None), P("sweep", None, None, None)),
        check_vma=False,
    )
```

```python
import math

import jax
import jax.numpy as jnp
from jax import lax
from jax.experimental import pallas as pl
from jax.experimental.pallas import tpu as pltpu
from jax.sharding import Mesh, PartitionSpec as P

NSEC = 32
WIDTH = 128
PAIRS = 128
ROWS = 3 * NSEC * WIDTH // 4
HALF = ROWS // 2
TOTAL = NSEC * WIDTH * WIDTH
X, ZL, ZH = 4, 4, 4
NEAR = ZL * X
PIECE = HALF // NEAR
SCALE = 1.0 / math.sqrt(PAIRS)
GROUP = 8
GROUPS = NSEC // GROUP
FIRST_GROUP = 16
REACH = NSEC - HALF // WIDTH
TAIL = 16
CHUNK = 256

VMEM = pl.BlockSpec(memory_space=pltpu.VMEM)
SMEM = pl.BlockSpec(memory_space=pltpu.SMEM)
HBM = pl.BlockSpec(memory_space=pltpu.HBM)
PACKED = pltpu.VMEM((ROWS + WIDTH, WIDTH), jnp.float32)
BLOCKS = pltpu.VMEM((NSEC, WIDTH, WIDTH), jnp.bfloat16)


def limit(mib):
    return pltpu.CompilerParams(vmem_limit_bytes=mib * 1024 * 1024)


def shape(dims, dtype):
    return jax.ShapeDtypeStruct(dims, dtype)


def square_mask(size):
    row = lax.broadcasted_iota(jnp.int32, (WIDTH, WIDTH), 0)
    col = lax.broadcasted_iota(jnp.int32, (WIDTH, WIDTH), 1)
    return (row < size) & (col < size)


def dot(a, b):
    return jnp.dot(a, b, preferred_element_type=jnp.float32)


def group_copies(pairs, sems, group=GROUP):
    return [
        [
            pltpu.make_async_copy(
                source.at[pl.ds(g * group, group)], target.at[pl.ds(g * group, group)], sems.at[g, k]
            )
            for k, (source, target) in enumerate(pairs)
        ]
        for g in range(NSEC // group)
    ]


def start_all(copies):
    for group in copies:
        for copy in group:
            copy.start()


def flat_sums(pairs):
    totals = None
    for start in range(0, ROWS, CHUNK):
        parts = [
            jnp.sum((p * q).reshape(CHUNK // 8, 8, WIDTH), axis=0)
            for p, q in pairs(pl.ds(start, CHUNK))
        ]
        totals = parts if totals is None else [t + p for t, p in zip(totals, parts)]
    return [jnp.sum(t, axis=(0, 1), keepdims=True) for t in totals]


def step_factors(x, sigma):
    def products(rows):
        xs, s = x[rows, :].astype(jnp.float32), sigma[rows, :].astype(jnp.float32)
        return [(xs, xs), (xs, s), (s, s)]

    xx, xs, ss = flat_sums(products)
    rho = xs / xx
    yy = xx + 0.64 * jnp.maximum(ss - rho * xs, 0.0)
    shrink = 1.0 / jnp.sqrt(yy / TOTAL + 1e-06)
    return (1.0 + 0.8 * rho) * shrink, 0.8 * shrink


def size_of(meta, i):
    return meta[2 + i]


def rows_below(size):
    return lax.broadcasted_iota(jnp.int32, (WIDTH, WIDTH), 0) < size


def run_pairs(meta, xb_of, left, right, env, group, ready, env_ready, packed, mine, other):
    sector = meta[1]
    column = lax.broadcasted_iota(jnp.int32, (WIDTH, WIDTH), 1)

    def body(g, carry):
        offset, at = carry
        ready(g)
        sums = []
        place = offset
        for j in range(group):
            i = g * group + j
            xb = xb_of(i, place)
            at = jnp.where(i == sector, place, at)
            place = place + size_of(meta, i)
            block = left[i]
            live = meta[2 + NSEC + i].astype(jnp.float32)
            u = live * dot(jnp.concatenate([block, block.T], 0), xb)
            u = u.astype(jnp.bfloat16)
            context = right[i]
            total = SCALE * dot(
                jnp.concatenate([u[:WIDTH], u[WIDTH:]], 1),
                jnp.concatenate([context.T, context], 0),
            )
            sums.append(jnp.where(column < size_of(meta, i), total, 0.0))
        for j in range(group):
            packed[pl.ds(offset, WIDTH), :] = sums[j]
            offset = offset + size_of(meta, g * group + j)
        return offset, at

    _, at = lax.fori_loop(0, NSEC // group, body, (jnp.int32(0), jnp.int32(0)))
    env_ready()
    term = 0.25 * dot(env[...], xb_of(sector, at, keep=False))
    packed[pl.ds(at, WIDTH), :] += jnp.where(square_mask(size_of(meta, sector)), term, 0.0)
    core = meta[0]
    mine[...] = packed[pl.ds(pl.multiple_of(core * HALF, 8), HALF), :]
    other[...] = packed[pl.ds(pl.multiple_of((1 - core) * HALF, 8), HALF), :].astype(jnp.bfloat16)


def first_kernel(
    meta, x0_in, left_in, right_in, env_in, mine, other, x_out,
    packed, x0, left, right, env, sems, env_sem, x_packed,
):
    pairs = [(x0_in, x0), (left_in, left), (right_in, right)]
    start_all(group_copies(pairs, sems, FIRST_GROUP))
    env_copy = pltpu.make_async_copy(env_in.at[meta[1]], env, env_sem.at[0])
    env_copy.start()

    def ready(g):
        some = pl.ds(g * FIRST_GROUP, FIRST_GROUP)
        for k, (source, target) in enumerate(pairs):
            pltpu.make_async_copy(source.at[some], target.at[some], sems.at[g, k]).wait()

    def xb_of(i, offset, keep=True):
        x = jnp.where(square_mask(size_of(meta, i)), x0[i].astype(jnp.float32), 0.0)
        if keep:
            x_packed[pl.ds(offset, WIDTH), :] = x
        return x.astype(jnp.bfloat16)

    run_pairs(meta, xb_of, left, right, env, FIRST_GROUP, ready, env_copy.wait, packed, mine, other)
    x_out[...] = x_packed[pl.ds(0, ROWS), :].astype(jnp.bfloat16)


def next_kernel(
    meta, sigma, x0, left, right, env_in, mine, other, wide, packed, env, env_sem
):
    env_copy = pltpu.make_async_copy(env_in.at[meta[1]], env, env_sem.at[0])
    env_copy.start()

    rows = pl.ds(0, ROWS)
    grow, drop = step_factors(x0, sigma)
    wide[rows, :] = grow * x0[...].astype(jnp.float32) - drop * sigma[...].astype(jnp.float32)

    def xb_of(i, offset, keep=True):
        mask = rows_below(size_of(meta, i))
        return jnp.where(mask, wide[pl.ds(offset, WIDTH), :], 0.0).astype(jnp.bfloat16)

    run_pairs(meta, xb_of, left, right, env, NSEC, lambda g: None, env_copy.wait, packed, mine, other)


def renorm_kernel(
    meta, x, sigma, env, factors_out, renorm_out, wide, packed
):
    grow, drop = step_factors(x, sigma)
    factors_out[0:1, :] = jnp.broadcast_to(grow, (1, WIDTH))
    factors_out[1:2, :] = jnp.broadcast_to(drop, (1, WIDTH))
    core = meta[0]
    near = pl.ds(pl.multiple_of(core * (HALF - WIDTH), 16), HALF + WIDTH)
    psi = grow * x[near, :] - drop * sigma[near, :].astype(jnp.float32)
    wide[near, :] = psi.astype(jnp.bfloat16).astype(jnp.float32)
    first = core * (NSEC - REACH)
    offset = lax.fori_loop(0, first, lambda i, total: total + size_of(meta, i), jnp.int32(0))
    blocks = []
    for j in range(REACH):
        i = first + j
        block = jnp.where(rows_below(size_of(meta, i)), wide[pl.ds(offset, WIDTH), :], 0.0)
        block = block.astype(jnp.bfloat16)
        applied = dot(env[i], block).astype(jnp.bfloat16)
        blocks.append((offset, dot(block.T, applied) / math.sqrt(WIDTH)))
        offset = offset + size_of(meta, i)
    for place, block in blocks:
        packed[pl.ds(place, WIDTH), :] = block
    renorm_out[pl.ds(0, HALF), :] = packed[
        pl.ds(pl.multiple_of(core * HALF, 8), HALF), :
    ].astype(jnp.bfloat16)
    lane = lax.broadcasted_iota(jnp.int32, (TAIL, WIDTH), 1)
    row = jnp.zeros((TAIL, WIDTH), jnp.int32)
    for i in range(NSEC):
        row = jnp.where(lane == i, size_of(meta, i), row)
    renorm_out[pl.ds(HALF, TAIL), :] = row.astype(jnp.float32).astype(jnp.bfloat16)


def unpack(size_at, wide, result, out, sems, finish):
    copies = group_copies([(result, out)], sems)
    offset = 0
    for g in range(GROUPS):
        for i in range(g * GROUP, (g + 1) * GROUP):
            size = size_at(i)
            block = jnp.where(rows_below(size), wide[pl.ds(offset, WIDTH), :], 0.0)
            result[i] = finish(i, block).astype(jnp.bfloat16)
            offset = offset + size
        copies[g][0].start()
    for group in copies:
        group[0].wait()


def psi_kernel(meta, factors, x, sigma, out, wide, result, sems):
    grow, drop = factors[0:1, :], factors[1:2, :]
    rows = pl.ds(0, ROWS)
    wide[rows, :] = grow * x[rows, :] - drop * sigma[...].astype(jnp.float32)
    unpack(lambda i: size_of(meta, i), wide, result, out, sems, lambda i, block: block)


def shift_kernel(came, env, out, wide, result, numbers, sizes, sems, own_sem):
    numbers[...] = came[pl.ds(HALF, TAIL), :].astype(jnp.float32).astype(jnp.int32)
    sizes_copy = pltpu.make_async_copy(numbers, sizes, own_sem.at[0])
    sizes_copy.start()
    wide[pl.ds(0, HALF), :] = came[pl.ds(0, HALF), :].astype(jnp.float32)
    wide[pl.ds(HALF, HALF), :] = came[pl.ds(HALF + TAIL, HALF), :].astype(jnp.float32)
    sizes_copy.wait()
    unpack(
        lambda i: sizes[0, i],
        wide,
        result,
        out,
        sems,
        lambda i, block: env[i].astype(jnp.float32) + block,
    )


def sum_kernel(parts, out):
    total = jnp.sum(parts[...].astype(jnp.float32), axis=0).astype(jnp.bfloat16)
    for k in range(out.shape[0]):
        out[k] = total


def summed(parts, copies):
    return pl.pallas_call(
        sum_kernel,
        in_specs=[VMEM],
        out_specs=VMEM,
        out_shape=shape((copies,) + parts.shape[1:], parts.dtype),
        compiler_params=limit(4),
    )(parts)


def exchange(value, axes):
    return lax.all_to_all(value, axes, 0, 0)


def all_summed(mine, other):
    both = lax.all_gather(other, "core")
    came = lax.dynamic_index_in_dim(both, 1 - lax.axis_index("core"), keepdims=False)
    chip = (mine + came.astype(jnp.float32)).astype(jnp.bfloat16).reshape(NEAR, PIECE, WIDTH)
    near = summed(exchange(chip, ("zl", "x")), ZH)
    far = summed(exchange(near, "zh"), NEAR)
    half = exchange(far, ("zl", "x"))
    return lax.all_gather(half.reshape(HALF, WIDTH), "core", tiled=True)


def dma(*dims):
    return pltpu.SemaphoreType.DMA(dims)


def shards(initial_trial_state, left_ops, right_ops, pair_sectors, sector_size, left_env):
    x0 = initial_trial_state[0]
    left = left_ops[0, 0]
    right = right_ops[0, 0]
    env = left_env[0]
    core = lax.axis_index("core")
    sector = lax.axis_index(("zh", "zl", "x", "core")) // (PAIRS // NSEC)
    own = jnp.stack([core, sector]).astype(jnp.int32)
    meta = jnp.concatenate([own, sector_size[0], pair_sectors[0, 0]])

    sums = [shape((HALF, WIDTH), jnp.float32), shape((HALF, WIDTH), jnp.bfloat16)]
    state = shape((ROWS + WIDTH, WIDTH), jnp.float32)
    blocks = shape((NSEC, WIDTH, WIDTH), jnp.bfloat16)
    env_scratch = [pltpu.VMEM((WIDTH, WIDTH), jnp.bfloat16)]
    mine, other, x0 = pl.pallas_call(
        first_kernel,
        in_specs=[SMEM] + [HBM] * 4,
        out_specs=[VMEM] * 3,
        out_shape=sums + [shape((ROWS, WIDTH), jnp.bfloat16)],
        scratch_shapes=[PACKED, BLOCKS, BLOCKS, BLOCKS]
        + env_scratch
        + [dma(NSEC // FIRST_GROUP, 3), dma(1), PACKED],
        compiler_params=limit(52),
    )(meta, x0, left, right, env)
    sigma = all_summed(mine, other)
    mine, other, x = pl.pallas_call(
        next_kernel,
        in_specs=[SMEM] + [VMEM] * 4 + [HBM],
        out_specs=[VMEM] * 3,
        out_shape=sums + [state],
        scratch_shapes=[PACKED] + env_scratch + [dma(1)],
        compiler_params=limit(12),
    )(meta, sigma, x0, left, right, env)
    sigma = all_summed(mine, other)
    factors, renorm = pl.pallas_call(
        renorm_kernel,
        in_specs=[SMEM] + [VMEM] * 3,
        out_specs=[VMEM] * 2,
        out_shape=[
            shape((2, WIDTH), jnp.float32),
            shape((HALF + TAIL, WIDTH), jnp.bfloat16),
        ],
        scratch_shapes=[PACKED, PACKED],
        compiler_params=limit(12),
    )(meta, x, sigma, env)
    positions = lax.axis_size("sweep")
    came = lax.ppermute(renorm, "sweep", [(i, i + 1) for i in range(positions - 1)])
    psi = pl.pallas_call(
        psi_kernel,
        in_specs=[SMEM] + [VMEM] * 3,
        out_specs=HBM,
        out_shape=blocks,
        scratch_shapes=[PACKED, BLOCKS, dma(GROUPS, 1)],
        compiler_params=limit(8),
        cost_estimate=pl.CostEstimate(flops=10**7, bytes_accessed=4 * 10**6, transcendentals=0),
    )(meta, factors, x, sigma)
    came = lax.all_gather(came, "core", tiled=True)
    next_left = pl.pallas_call(
        shift_kernel,
        in_specs=[VMEM] * 2,
        out_specs=HBM,
        out_shape=blocks,
        scratch_shapes=[
            PACKED,
            BLOCKS,
            pltpu.VMEM((TAIL, WIDTH), jnp.int32),
            pltpu.SMEM((TAIL, WIDTH), jnp.int32),
            dma(GROUPS, 1),
            dma(1),
        ],
        compiler_params=limit(8),
    )(came, env)
    return psi[None], next_left[None]


def solution(mesh):
    positions = mesh.shape["sweep"]
    split = Mesh(
        mesh.devices.reshape(positions, ZH, ZL, X, 2), ("sweep", "zh", "zl", "x", "core")
    )
    ops = ("zh", "zl", "x", "core")
    return jax.shard_map(
        shards,
        mesh=split,
        in_specs=(
            P("sweep", None, None, None),
            P("sweep", ops, None, None, None),
            P("sweep", ops, None, None, None),
            P("sweep", ops, None),
            P("sweep", None),
            P("sweep", None, None, None),
        ),
        out_specs=(P("sweep", None, None, None), P("sweep", None, None, None)),
        check_vma=False,
    )
```

```python
import math

import jax
import jax.numpy as jnp
from jax import lax
from jax.experimental import pallas as pl
from jax.experimental.pallas import tpu as pltpu
from jax.sharding import Mesh, PartitionSpec as P

NSEC = 32
WIDTH = 128
PAIRS = 128
ROWS = 3 * NSEC * WIDTH // 4
HALF = ROWS // 2
TOTAL = NSEC * WIDTH * WIDTH
X, ZL, ZH = 4, 4, 4
NEAR = ZL * X
PIECE = HALF // NEAR
SCALE = 1.0 / math.sqrt(PAIRS)
GROUP = 8
GROUPS = NSEC // GROUP
FIRST_GROUP = 16
REACH = NSEC - HALF // WIDTH
TAIL = 16
CHUNK = 256

VMEM = pl.BlockSpec(memory_space=pltpu.VMEM)
SMEM = pl.BlockSpec(memory_space=pltpu.SMEM)
HBM = pl.BlockSpec(memory_space=pltpu.HBM)
PACKED = pltpu.VMEM((ROWS + WIDTH, WIDTH), jnp.float32)
BLOCKS = pltpu.VMEM((NSEC, WIDTH, WIDTH), jnp.bfloat16)


def limit(mib):
    return pltpu.CompilerParams(vmem_limit_bytes=mib * 1024 * 1024)


def shape(dims, dtype):
    return jax.ShapeDtypeStruct(dims, dtype)


def square_mask(size):
    row = lax.broadcasted_iota(jnp.int32, (WIDTH, WIDTH), 0)
    col = lax.broadcasted_iota(jnp.int32, (WIDTH, WIDTH), 1)
    return (row < size) & (col < size)


def dot(a, b):
    return jnp.dot(a, b, preferred_element_type=jnp.float32)


def group_copies(pairs, sems, group=GROUP):
    return [
        [
            pltpu.make_async_copy(
                source.at[pl.ds(g * group, group)], target.at[pl.ds(g * group, group)], sems.at[g, k]
            )
            for k, (source, target) in enumerate(pairs)
        ]
        for g in range(NSEC // group)
    ]


def start_all(copies):
    for group in copies:
        for copy in group:
            copy.start()


def flat_sums(pairs):
    totals = None
    for start in range(0, ROWS, CHUNK):
        parts = [
            jnp.sum((p * q).reshape(CHUNK // 8, 8, WIDTH), axis=0)
            for p, q in pairs(pl.ds(start, CHUNK))
        ]
        totals = parts if totals is None else [t + p for t, p in zip(totals, parts)]
    return [jnp.sum(t, axis=(0, 1), keepdims=True) for t in totals]


def step_factors(x, sigma):
    def products(rows):
        xs, s = x[rows, :].astype(jnp.float32), sigma[rows, :].astype(jnp.float32)
        return [(xs, xs), (xs, s), (s, s)]

    xx, xs, ss = flat_sums(products)
    rho = xs / xx
    yy = xx + 0.64 * jnp.maximum(ss - rho * xs, 0.0)
    shrink = 1.0 / jnp.sqrt(yy / TOTAL + 1e-06)
    return (1.0 + 0.8 * rho) * shrink, 0.8 * shrink


def size_of(meta, i):
    return meta[2 + i]


def rows_below(size):
    return lax.broadcasted_iota(jnp.int32, (WIDTH, WIDTH), 0) < size


def run_pairs(meta, xb_of, left, right, env_block, group, ready, packed, mine, other):
    sector = meta[1]
    column = lax.broadcasted_iota(jnp.int32, (WIDTH, WIDTH), 1)

    def body(g, carry):
        offset, at = carry
        ready(g)
        sums = []
        place = offset
        for j in range(group):
            i = g * group + j
            xb = xb_of(i, place)
            at = jnp.where(i == sector, place, at)
            place = place + size_of(meta, i)
            block = left[i]
            live = meta[2 + NSEC + i].astype(jnp.float32)
            u = live * dot(jnp.concatenate([block, block.T], 0), xb)
            u = u.astype(jnp.bfloat16)
            context = right[i]
            total = SCALE * dot(
                jnp.concatenate([u[:WIDTH], u[WIDTH:]], 1),
                jnp.concatenate([context.T, context], 0),
            )
            sums.append(jnp.where(column < size_of(meta, i), total, 0.0))
        for j in range(group):
            packed[pl.ds(offset, WIDTH), :] = sums[j]
            offset = offset + size_of(meta, g * group + j)
        return offset, at

    _, at = lax.fori_loop(0, NSEC // group, body, (jnp.int32(0), jnp.int32(0)))
    term = 0.25 * dot(env_block(), xb_of(sector, at, keep=False))
    packed[pl.ds(at, WIDTH), :] += jnp.where(square_mask(size_of(meta, sector)), term, 0.0)
    core = meta[0]
    mine[...] = packed[pl.ds(pl.multiple_of(core * HALF, 8), HALF), :]
    other[...] = packed[pl.ds(pl.multiple_of((1 - core) * HALF, 8), HALF), :].astype(jnp.bfloat16)


def first_kernel(
    meta, x0_in, left_in, right_in, env_in, mine, other, x_out,
    packed, x0, left, right, env, sems, env_sem, x_packed,
):
    pairs = [(x0_in, x0), (left_in, left), (right_in, right)]
    start_all(group_copies(pairs, sems, FIRST_GROUP))
    env_copy = pltpu.make_async_copy(env_in.at[meta[1]], env, env_sem.at[0])
    env_copy.start()

    def ready(g):
        some = pl.ds(g * FIRST_GROUP, FIRST_GROUP)
        for k, (source, target) in enumerate(pairs):
            pltpu.make_async_copy(source.at[some], target.at[some], sems.at[g, k]).wait()

    def xb_of(i, offset, keep=True):
        x = jnp.where(square_mask(size_of(meta, i)), x0[i].astype(jnp.float32), 0.0)
        if keep:
            x_packed[pl.ds(offset, WIDTH), :] = x
        return x.astype(jnp.bfloat16)

    def env_block():
        env_copy.wait()
        return env[...]

    run_pairs(meta, xb_of, left, right, env_block, FIRST_GROUP, ready, packed, mine, other)
    x_out[...] = x_packed[pl.ds(0, ROWS), :].astype(jnp.bfloat16)


def next_kernel(
    meta, sigma, x0, left, right, env, mine, other, wide, packed
):
    rows = pl.ds(0, ROWS)
    grow, drop = step_factors(x0, sigma)
    wide[rows, :] = grow * x0[...].astype(jnp.float32) - drop * sigma[...].astype(jnp.float32)

    def xb_of(i, offset, keep=True):
        mask = rows_below(size_of(meta, i))
        return jnp.where(mask, wide[pl.ds(offset, WIDTH), :], 0.0).astype(jnp.bfloat16)

    run_pairs(
        meta, xb_of, left, right, lambda: env[meta[1]], NSEC, lambda g: None, packed, mine, other
    )


def renorm_kernel(
    meta, x, sigma, env, factors_out, renorm_out, wide, packed
):
    grow, drop = step_factors(x, sigma)
    factors_out[0:1, :] = jnp.broadcast_to(grow, (1, WIDTH))
    factors_out[1:2, :] = jnp.broadcast_to(drop, (1, WIDTH))
    core = meta[0]
    near = pl.ds(pl.multiple_of(core * (HALF - WIDTH), 16), HALF + WIDTH)
    psi = grow * x[near, :] - drop * sigma[near, :].astype(jnp.float32)
    wide[near, :] = psi.astype(jnp.bfloat16).astype(jnp.float32)
    first = core * (NSEC - REACH)
    offset = lax.fori_loop(0, first, lambda i, total: total + size_of(meta, i), jnp.int32(0))
    blocks = []
    for j in range(REACH):
        i = first + j
        block = jnp.where(rows_below(size_of(meta, i)), wide[pl.ds(offset, WIDTH), :], 0.0)
        block = block.astype(jnp.bfloat16)
        applied = dot(env[i], block).astype(jnp.bfloat16)
        blocks.append((offset, dot(block.T, applied) / math.sqrt(WIDTH)))
        offset = offset + size_of(meta, i)
    for place, block in blocks:
        packed[pl.ds(place, WIDTH), :] = block
    renorm_out[pl.ds(0, HALF), :] = packed[
        pl.ds(pl.multiple_of(core * HALF, 8), HALF), :
    ].astype(jnp.bfloat16)
    lane = lax.broadcasted_iota(jnp.int32, (TAIL, WIDTH), 1)
    row = jnp.zeros((TAIL, WIDTH), jnp.int32)
    for i in range(NSEC):
        row = jnp.where(lane == i, size_of(meta, i), row)
    renorm_out[pl.ds(HALF, TAIL), :] = row.astype(jnp.float32).astype(jnp.bfloat16)


def unpack(size_at, wide, result, out, sems, finish):
    copies = group_copies([(result, out)], sems)
    offset = 0
    for g in range(GROUPS):
        for i in range(g * GROUP, (g + 1) * GROUP):
            size = size_at(i)
            block = jnp.where(rows_below(size), wide[pl.ds(offset, WIDTH), :], 0.0)
            result[i] = finish(i, block).astype(jnp.bfloat16)
            offset = offset + size
        copies[g][0].start()
    for group in copies:
        group[0].wait()


def psi_kernel(meta, factors, x, sigma, out, wide, result, sems):
    grow, drop = factors[0:1, :], factors[1:2, :]
    rows = pl.ds(0, ROWS)
    wide[rows, :] = grow * x[rows, :] - drop * sigma[...].astype(jnp.float32)
    unpack(lambda i: size_of(meta, i), wide, result, out, sems, lambda i, block: block)


def shift_kernel(came, env, out, wide, result, numbers, sizes, sems, own_sem):
    numbers[...] = came[pl.ds(HALF, TAIL), :].astype(jnp.float32).astype(jnp.int32)
    sizes_copy = pltpu.make_async_copy(numbers, sizes, own_sem.at[0])
    sizes_copy.start()
    wide[pl.ds(0, HALF), :] = came[pl.ds(0, HALF), :].astype(jnp.float32)
    wide[pl.ds(HALF, HALF), :] = came[pl.ds(HALF + TAIL, HALF), :].astype(jnp.float32)
    sizes_copy.wait()
    unpack(
        lambda i: sizes[0, i],
        wide,
        result,
        out,
        sems,
        lambda i, block: env[i].astype(jnp.float32) + block,
    )


def sum_kernel(parts, out):
    total = jnp.sum(parts[...].astype(jnp.float32), axis=0).astype(jnp.bfloat16)
    for k in range(out.shape[0]):
        out[k] = total


def summed(parts, copies):
    return pl.pallas_call(
        sum_kernel,
        in_specs=[VMEM],
        out_specs=VMEM,
        out_shape=shape((copies,) + parts.shape[1:], parts.dtype),
        compiler_params=limit(4),
    )(parts)


def exchange(value, axes):
    return lax.all_to_all(value, axes, 0, 0)


def all_summed(mine, other):
    both = lax.all_gather(other, "core")
    came = lax.dynamic_index_in_dim(both, 1 - lax.axis_index("core"), keepdims=False)
    chip = (mine + came.astype(jnp.float32)).astype(jnp.bfloat16).reshape(NEAR, PIECE, WIDTH)
    near = summed(exchange(chip, ("zl", "x")), ZH)
    far = summed(exchange(near, "zh"), NEAR)
    half = exchange(far, ("zl", "x"))
    return lax.all_gather(half.reshape(HALF, WIDTH), "core", tiled=True)


def dma(*dims):
    return pltpu.SemaphoreType.DMA(dims)


def shards(initial_trial_state, left_ops, right_ops, pair_sectors, sector_size, left_env):
    x0 = initial_trial_state[0]
    left = left_ops[0, 0]
    right = right_ops[0, 0]
    env = left_env[0]
    core = lax.axis_index("core")
    sector = lax.axis_index(("zh", "zl", "x", "core")) // (PAIRS // NSEC)
    own = jnp.stack([core, sector]).astype(jnp.int32)
    meta = jnp.concatenate([own, sector_size[0], pair_sectors[0, 0]])

    sums = [shape((HALF, WIDTH), jnp.float32), shape((HALF, WIDTH), jnp.bfloat16)]
    state = shape((ROWS + WIDTH, WIDTH), jnp.float32)
    blocks = shape((NSEC, WIDTH, WIDTH), jnp.bfloat16)
    env_scratch = [pltpu.VMEM((WIDTH, WIDTH), jnp.bfloat16)]
    mine, other, x0 = pl.pallas_call(
        first_kernel,
        in_specs=[SMEM] + [HBM] * 4,
        out_specs=[VMEM] * 3,
        out_shape=sums + [shape((ROWS, WIDTH), jnp.bfloat16)],
        scratch_shapes=[PACKED, BLOCKS, BLOCKS, BLOCKS]
        + env_scratch
        + [dma(NSEC // FIRST_GROUP, 3), dma(1), PACKED],
        compiler_params=limit(52),
    )(meta, x0, left, right, env)
    sigma = all_summed(mine, other)
    mine, other, x = pl.pallas_call(
        next_kernel,
        in_specs=[SMEM] + [VMEM] * 5,
        out_specs=[VMEM] * 3,
        out_shape=sums + [state],
        scratch_shapes=[PACKED],
        compiler_params=limit(12),
    )(meta, sigma, x0, left, right, env)
    sigma = all_summed(mine, other)
    factors, renorm = pl.pallas_call(
        renorm_kernel,
        in_specs=[SMEM] + [VMEM] * 3,
        out_specs=[VMEM] * 2,
        out_shape=[
            shape((2, WIDTH), jnp.float32),
            shape((HALF + TAIL, WIDTH), jnp.bfloat16),
        ],
        scratch_shapes=[PACKED, PACKED],
        compiler_params=limit(12),
    )(meta, x, sigma, env)
    positions = lax.axis_size("sweep")
    came = lax.ppermute(renorm, "sweep", [(i, i + 1) for i in range(positions - 1)])
    psi = pl.pallas_call(
        psi_kernel,
        in_specs=[SMEM] + [VMEM] * 3,
        out_specs=HBM,
        out_shape=blocks,
        scratch_shapes=[PACKED, BLOCKS, dma(GROUPS, 1)],
        compiler_params=limit(8),
        cost_estimate=pl.CostEstimate(flops=10**7, bytes_accessed=4 * 10**6, transcendentals=0),
    )(meta, factors, x, sigma)
    came = lax.all_gather(came, "core", tiled=True)
    next_left = pl.pallas_call(
        shift_kernel,
        in_specs=[VMEM] * 2,
        out_specs=HBM,
        out_shape=blocks,
        scratch_shapes=[
            PACKED,
            BLOCKS,
            pltpu.VMEM((TAIL, WIDTH), jnp.int32),
            pltpu.SMEM((TAIL, WIDTH), jnp.int32),
            dma(GROUPS, 1),
            dma(1),
        ],
        compiler_params=limit(8),
    )(came, env)
    return psi[None], next_left[None]


def solution(mesh):
    positions = mesh.shape["sweep"]
    split = Mesh(
        mesh.devices.reshape(positions, ZH, ZL, X, 2), ("sweep", "zh", "zl", "x", "core")
    )
    ops = ("zh", "zl", "x", "core")
    return jax.shard_map(
        shards,
        mesh=split,
        in_specs=(
            P("sweep", None, None, None),
            P("sweep", ops, None, None, None),
            P("sweep", ops, None, None, None),
            P("sweep", ops, None),
            P("sweep", None),
            P("sweep", None, None, None),
        ),
        out_specs=(P("sweep", None, None, None), P("sweep", None, None, None)),
        check_vma=False,
    )
```
